32 devices in a mesh: slab: 2 (over y), curve: 4 (over z), node: 2 (over x), sub: 2 (over core).
Axes of the slice: x: 2, y: 2, z: 4, core: 2. Of those that a mesh axis runs over, the one named last changes fastest.
Arguments:
- start_field: float32 [128, 16, 256], P(('slab', 'curve', 'sub')), parts along dimension 0, may hold values from -1 to 1
- neighbours: int32 [128, 6], P(('slab', 'curve', 'sub')), parts along dimension 0, may hold values from -1 to 63, as said below
Outputs:
- node_fields: float32 [2, 128, 16, 256], P('node', ('slab', 'curve', 'sub')), parts along dimension 1
- increments: float32 [4, 2], P('slab', 'node'), parts along dimension 0
The draws below stay inside these ranges and needn't reach their ends.
There are 2 independent parts, one for each index of `slab`. The reference program is written for one: setup_inputs(seed, part) draws one part's arguments, and reference() takes and returns one part's arrays. A program takes and returns all parts, laid end to end along the dimension named above; each array names one. Nothing has to cross between parts.
Inputs may be any that keep to these rules, and one draw needn't show every extreme that they name: Leaf block c lies in layer c // 8 of the slab's first dimension; each layer holds 4 x 2 blocks visited in an order drawn per layer. The -x and +x neighbours lie in the adjacent layers, the others in the own layer. Where a block names b across a face, b names that block across the opposite face.
All inputs are finite; a program needn't handle non-finite values.
Results may differ from the reference program's by a relative error of at most 0.0001.
Values sent between devices are 32-bit elements; how exact they have to be, the bound alone decides.
No kernel may reach another device: no remote copies, remote signals or barrier semaphores. Data moves between devices by JAX's collectives and lax.ppermute only.
A program may use at most 64 MiB of HBM per device.

```python
import jax
import jax.numpy as jnp
import numpy as np

EDGE = 16
SPAN_Y = 4
SPAN_Z = 2
SWEEPS = 2
JACOBI = 4
BLK_DEV = 8
NBLK = 64
N_NODE = 2


def draw_start_field(key, part):
    key = jax.random.fold_in(key, 5)
    layers = NBLK // BLK_DEV
    position = jnp.arange(NBLK)[:, None, None] // BLK_DEV * EDGE + jnp.arange(EDGE)[None, :, None]
    amplitude = jnp.exp(jnp.log(3.0) * (position.astype(jnp.float32) / (layers * EDGE - 1) - 1.0))
    uniform_part = jax.random.uniform(key, (NBLK, EDGE, EDGE * EDGE), jnp.float32, -1.0, 1.0)
    values = amplitude * uniform_part
    return values


def draw_neighbours(key, part):
    key = jax.random.fold_in(key, 7)
    layers = NBLK // BLK_DEV
    layer_keys = jax.random.split(key, layers)
    orders = jax.vmap(lambda single: jax.random.permutation(single, BLK_DEV))(layer_keys).astype(jnp.int32)
    slots = jnp.argsort(orders, axis=1).astype(jnp.int32)
    layer_index = jnp.arange(layers, dtype=jnp.int32)[:, None] + jnp.zeros((1, BLK_DEV), jnp.int32)
    places = orders
    across_y = places // SPAN_Z
    across_z = places % SPAN_Z

    def locate(target_layer, target_place):
        safe_layer = jnp.clip(target_layer, 0, layers - 1)
        safe_place = jnp.clip(target_place, 0, BLK_DEV - 1)
        return safe_layer * BLK_DEV + slots[safe_layer, safe_place]
    minus_x = jnp.where(layer_index > 0, locate(layer_index - 1, places), -1)
    plus_x = jnp.where(layer_index < layers - 1, locate(layer_index + 1, places), -1)
    minus_y = jnp.where(across_y > 0, locate(layer_index, places - SPAN_Z), -1)
    plus_y = jnp.where(across_y < SPAN_Y - 1, locate(layer_index, places + SPAN_Z), -1)
    minus_z = jnp.where(across_z > 0, locate(layer_index, places - 1), -1)
    plus_z = jnp.where(across_z < SPAN_Z - 1, locate(layer_index, places + 1), -1)
    stacked = jnp.stack([minus_x, plus_x, minus_y, plus_y, minus_z, plus_z], axis=-1)
    return stacked.reshape(NBLK, 6).astype(jnp.int32)


def setup_inputs(seed: int = 0, part: int = 0) -> dict:
    keys = jax.random.split(jax.random.key(seed), 3)
    own_keys = jax.random.split(jax.random.fold_in(keys[2], part), 3)
    start_field = draw_start_field(jax.random.fold_in(jax.random.fold_in(keys[2], part), 71), part)
    neighbours = draw_neighbours(jax.random.fold_in(jax.random.fold_in(keys[2], part), 71), part)
    return {"start_field": start_field, "neighbours": neighbours}


diffusion = 0.5
reaction = 1.0
opposite = (1, 0, 3, 2, 5, 4)

def legendre_value(order, place):
    before = 1.0
    if order == 0:
        return before
    current = place
    for degree in range(1, order):
        following = ((2 * degree + 1) * place * current - degree * before) / (degree + 1)
        before = current
        current = following
    return current

def radau_residue(node_count, moment):
    place = 2.0 * moment - 1.0
    return legendre_value(node_count, place) - legendre_value(node_count - 1, place)

def radau_tables(node_count):
    samples = 4000
    points = []
    for sample in range(samples - 1):
        left_end = sample / samples
        right_end = (sample + 1) / samples
        left_value = radau_residue(node_count, left_end)
        right_value = radau_residue(node_count, right_end)
        if left_value * right_value < 0.0:
            for halving in range(80):
                middle = 0.5 * (left_end + right_end)
                middle_value = radau_residue(node_count, middle)
                if left_value * middle_value <= 0.0:
                    right_end = middle
                else:
                    left_end = middle
                    left_value = middle_value
            points.append(0.5 * (left_end + right_end))
    points.append(1.0)
    table = []
    for row_node in range(node_count):
        table_row = []
        for col_node in range(node_count):
            factors = [1.0]
            for other_node in range(node_count):
                if other_node != col_node:
                    scale = 1.0 / (points[col_node] - points[other_node])
                    shifted = [0.0] + factors
                    product = [shifted[place] - points[other_node] * (factors[place] if place < len(factors) else 0.0) for place in range(len(shifted))]
                    factors = [entry * scale for entry in product]
            integral = 0.0
            for power_index in range(len(factors)):
                integral = integral + factors[power_index] * points[row_node] ** (power_index + 1) / (power_index + 1)
            table_row.append(integral)
        table.append(table_row)
    return (np.array(table, dtype=np.float32), np.array(points, dtype=np.float32))

def face_stack(block_field):
    edge_cells = block_field.shape[1]
    block_count = block_field.shape[0]
    low_x = block_field[:, 0, :]
    high_x = block_field[:, -1, :]
    low_y = block_field[:, :, :edge_cells].reshape(block_count, -1)
    high_y = block_field[:, :, -edge_cells:].reshape(block_count, -1)
    low_z = block_field[:, :, 0::edge_cells].reshape(block_count, -1)
    high_z = block_field[:, :, edge_cells - 1::edge_cells].reshape(block_count, -1)
    return jnp.stack([low_x, high_x, low_y, high_y, low_z, high_z], axis=1)

def assemble(block_field, ghost_faces):
    edge_cells = block_field.shape[1]
    block_count = block_field.shape[0]
    plane_cells = block_field.shape[2]
    padded = jnp.concatenate([ghost_faces[:, 0][:, None], block_field, ghost_faces[:, 1][:, None]], axis=1)
    totals = padded[:, :-2] + padded[:, 2:]
    below_y = jnp.concatenate([ghost_faces[:, 2].reshape(block_count, edge_cells, edge_cells), block_field[:, :, :-edge_cells]], axis=-1)
    above_y = jnp.concatenate([block_field[:, :, edge_cells:], ghost_faces[:, 3].reshape(block_count, edge_cells, edge_cells)], axis=-1)
    totals = totals + below_y + above_y
    within = jnp.arange(plane_cells, dtype=jnp.int32) % edge_cells
    lower_face = jnp.repeat(ghost_faces[:, 4].reshape(block_count, edge_cells, edge_cells), edge_cells, axis=-1)
    upper_face = jnp.repeat(ghost_faces[:, 5].reshape(block_count, edge_cells, edge_cells), edge_cells, axis=-1)
    totals = totals + jnp.where(within == 0, lower_face, jnp.roll(block_field, 1, axis=-1))
    totals = totals + jnp.where(within == edge_cells - 1, upper_face, jnp.roll(block_field, -1, axis=-1))
    return totals

def reference_sum(block_field, neighbours):
    block_count = block_field.shape[0]
    own_faces = face_stack(block_field)
    own_rows = jnp.arange(block_count, dtype=jnp.int32)[:, None] + jnp.zeros((1, 6), jnp.int32)
    sides = jnp.arange(6, dtype=jnp.int32)[None, :] + jnp.zeros((block_count, 1), jnp.int32)
    present = neighbours >= 0
    source_rows = jnp.where(present, neighbours, own_rows)
    source_cols = jnp.where(present, jnp.asarray(opposite, dtype=jnp.int32)[None, :], sides)
    ghost_faces = own_faces[source_rows, source_cols]
    return assemble(block_field, ghost_faces)

def reference(start_field, neighbours):
    weights, points = radau_tables(N_NODE)
    fields_list = [start_field for node_index in range(N_NODE)]
    total_cells = start_field.size
    increment_rows = []
    for sweep_index in range(SWEEPS):
        around_list = [reference_sum(values, neighbours) for values in fields_list]
        laplace_list = [around_list[node_index] - 6.0 * fields_list[node_index] for node_index in range(N_NODE)]
        forces = [diffusion * laplace_list[node_index] + reaction * fields_list[node_index] * (1.0 - fields_list[node_index] * fields_list[node_index]) for node_index in range(N_NODE)]
        norm_row = []
        new_fields = []
        for node_index in range(N_NODE):
            stiffness = jnp.float32(diffusion) * jnp.asarray(points)[node_index]
            integral = jnp.zeros_like(start_field)
            for other_index in range(N_NODE):
                integral = integral + jnp.asarray(weights)[node_index, other_index] * forces[other_index]
            right_side = start_field + integral - stiffness * laplace_list[node_index]
            update = fields_list[node_index]
            neighbour_total = around_list[node_index]
            for jacobi_index in range(JACOBI):
                update = (right_side + stiffness * neighbour_total) / (1.0 + 6.0 * stiffness)
                if jacobi_index + 1 < JACOBI:
                    neighbour_total = reference_sum(update, neighbours)
            change = update - fields_list[node_index]
            norm_row.append(jnp.sqrt(jnp.sum(change * change) / total_cells + 1e-06))
            new_fields.append(update)
        fields_list = new_fields
        increment_rows.append(jnp.stack(norm_row))
    return (jnp.stack(fields_list), jnp.stack(increment_rows))
```

```python
import functools

import jax
import jax.numpy as jnp
import numpy as np
from jax import lax
from jax.experimental import pallas as pl
from jax.experimental.pallas import tpu as pltpu
from jax.sharding import PartitionSpec as P

SWEEPS = 2
JACOBI = 4

diffusion = 0.5
reaction = 1.0
EDGE = 16
SPAN_Z = 2
LANES = 128
GROUP = SPAN_Z * EDGE
HALO = 8
PAD = 8
WIDTH = EDGE + 2 * HALO
ROWS = WIDTH + 2 * PAD
VMEM = pl.BlockSpec(memory_space=pltpu.VMEM)
SMEM = pl.BlockSpec(memory_space=pltpu.SMEM)


def legendre_value(order, place):
    before = 1.0
    current = place
    for degree in range(1, order):
        following = ((2 * degree + 1) * place * current - degree * before) / (degree + 1)
        before = current
        current = following
    return current


def radau_residue(node_count, moment):
    place = 2.0 * moment - 1.0
    return legendre_value(node_count, place) - legendre_value(node_count - 1, place)


def radau_tables(node_count):
    samples = 4000
    points = []
    for sample in range(samples - 1):
        left_end = sample / samples
        right_end = (sample + 1) / samples
        left_value = radau_residue(node_count, left_end)
        right_value = radau_residue(node_count, right_end)
        if left_value * right_value < 0.0:
            for halving in range(80):
                middle = 0.5 * (left_end + right_end)
                middle_value = radau_residue(node_count, middle)
                if left_value * middle_value <= 0.0:
                    right_end = middle
                else:
                    left_end = middle
                    left_value = middle_value
            points.append(0.5 * (left_end + right_end))
    points.append(1.0)
    table = []
    for row_node in range(node_count):
        table_row = []
        for col_node in range(node_count):
            factors = [1.0]
            for other_node in range(node_count):
                if other_node != col_node:
                    scale = 1.0 / (points[col_node] - points[other_node])
                    shifted = [0.0] + factors
                    product = [
                        shifted[place]
                        - points[other_node] * (factors[place] if place < len(factors) else 0.0)
                        for place in range(len(shifted))
                    ]
                    factors = [entry * scale for entry in product]
            integral = 0.0
            for power_index in range(len(factors)):
                integral = integral + factors[power_index] * points[row_node] ** (
                    power_index + 1
                ) / (power_index + 1)
            table_row.append(integral)
        table.append(table_row)
    return (np.array(table, dtype=np.float32), np.array(points, dtype=np.float32))


def slots_by_place(table):
    count = 8
    corner = jnp.int32(0)
    for slot in range(count):
        lowest = jnp.logical_and(table[slot, 2] < 0, table[slot, 4] < 0)
        corner = jnp.where(lowest, jnp.int32(slot), corner)
    slots = []
    for across_y in range(count // SPAN_Z):
        slots.append(corner)
        slots.append(table[corner, 5] & (count - 1))
        if across_y + 1 < count // SPAN_Z:
            corner = table[corner, 3] & (count - 1)
    return slots


def transpose_granules(values):
    lane = lax.broadcasted_iota(jnp.int32, (8, LANES), 1)
    for bit in (4, 2, 1):
        high = (lane // EDGE) & bit != 0
        out = list(values)
        for first in range(8):
            if first & bit == 0:
                low_value, high_value = values[first], values[first + bit]
                out[first] = jnp.where(high, pltpu.roll(high_value, EDGE * bit, 1), low_value)
                out[first + bit] = jnp.where(
                    high, high_value, pltpu.roll(low_value, LANES - EDGE * bit, 1)
                )
        values = out
    return values


def split_kernel(field, table, chip_half, far_half):
    sub = lax.axis_index("sub")
    slots = slots_by_place(table)
    for target, start in ((far_half, sub * 8), (chip_half, 8 - sub * 8)):
        rows = pl.ds(pl.multiple_of(start, 8), 8)
        for side in range(2):
            columns = slice(side * LANES, (side + 1) * LANES)
            values = transpose_granules([field[slot, rows, columns] for slot in slots])
            for row, value in enumerate(values):
                target[side * 8 + row] = value


def merge_kernel(planes, table, field):
    slots = slots_by_place(table)
    for half in range(2):
        rows = slice(half * 8, half * 8 + 8)
        for side in range(2):
            columns = slice(side * LANES, (side + 1) * LANES)
            values = transpose_granules([planes[side * 8 + row, rows] for row in range(8)])
            for slot, value in zip(slots, values):
                field[0, slot, rows, columns] = value


def chunks(level):
    count = -(-(WIDTH - 2 * level) // 8)
    first = (WIDTH - 8 * count) // 2
    return [PAD + first + 8 * piece for piece in range(count)]


def around(source, start, masks):
    at_low, at_high, first_group, last_group = masks
    rows = pl.ds(start, 8)
    below_rows = pl.ds(start - 1, 8)
    above_rows = pl.ds(start + 1, 8)
    first = source[0, rows]
    last = source[EDGE - 1, rows]
    before = jnp.where(first_group, first, pltpu.roll(last, GROUP, 1))
    beyond = jnp.where(last_group, last, pltpu.roll(first, LANES - GROUP, 1))
    current = first
    for j in range(EDGE):
        if j + 1 < EDGE:
            following = source[j + 1, rows]
        else:
            following = beyond
        total = (source[j, below_rows] + source[j, above_rows]) + (before + following)
        total = total + jnp.where(at_low, current, pltpu.roll(current, 1, 1))
        total = total + jnp.where(at_high, current, pltpu.roll(current, LANES - 1, 1))
        yield j, current, total
        before, current = current, following


def sweep_kernel(
    nodes, weights, points, chip_half, far_half, chip_got, far_got, planes, sums, base, state, right, after
):
    sub = lax.axis_index("sub")
    curve = lax.axis_index("curve")
    node = lax.axis_index("node")
    layer = curve * lax.axis_size("sub") + sub
    layers = lax.axis_size("curve") * lax.axis_size("sub")
    at_end = jnp.logical_or(layer == 0, layer == layers - 1)
    flip = sub == 1

    def place(source, normal, flipped):
        start = pl.multiple_of(PAD + jnp.where(flip, flipped, normal), 8)
        base[:, pl.ds(start, 8), :] = source[...]

    place(far_half, 8, 16)
    place(chip_half, 16, 8)
    place(chip_got, 24, 0)

    @pl.when(jnp.logical_not(at_end))
    def _():
        place(far_got, 0, 24)

    @pl.when(at_end)
    def _():
        start = PAD + jnp.where(flip, 24, 0)
        for row in range(8):
            base[:, pl.ds(start + 7 - row, 1), :] = far_half[:, row : row + 1, :]

    lane = lax.broadcasted_iota(jnp.int32, (8, LANES), 1)
    masks = (
        lane % GROUP == 0,
        lane % GROUP == GROUP - 1,
        lane < GROUP,
        lane >= LANES - GROUP,
    )
    stiffness = [np.float32(diffusion) * points[n] for n in range(nodes)]
    scales = [np.float32(1.0) / (np.float32(1.0) + np.float32(6.0) * a) for a in stiffness]
    whole = [np.float32(np.sum(weights[n].astype(np.float64))) for n in range(nodes)]

    for start in chunks(1):
        rows = pl.ds(start, 8)
        for j, value, total in around(base, start, masks):
            laplace = total - 6.0 * value
            force = diffusion * laplace + reaction * value * (1.0 - value * value)
            for n in range(nodes):
                right[n, j, rows] = (value + whole[n] * force - stiffness[n] * laplace) * scales[n]
                state[n, j, rows] = value + (whole[n] * scales[n]) * force
    for n in range(nodes):
        source, target = state.at[n], after.at[n]
        for level in range(2, JACOBI + 1):
            for start in chunks(level):
                rows = pl.ds(start, 8)
                for j, value, total in around(source, start, masks):
                    target[j, rows] = right[n, j, rows] + (stiffness[n] * scales[n]) * total
            source, target = target, source

    def own(values):
        chosen = jnp.float32(values[0])
        for n in range(1, nodes):
            chosen = jnp.where(node == n, jnp.float32(values[n]), chosen)
        return chosen

    own_stiffness = own(stiffness)
    own_scale = own(scales)
    own_weights = [own([weights[m, n] for m in range(nodes)]) for n in range(nodes)]
    fields = after if JACOBI % 2 == 0 else state
    spare = state if JACOBI % 2 == 0 else after
    for start in chunks(JACOBI + 1):
        rows = pl.ds(start, 8)
        for steps in zip(*[around(fields.at[n], start, masks) for n in range(nodes)]):
            j = steps[0][0]
            integral = base[j, rows]
            own_value = steps[0][1]
            own_laplace = None
            for n, (_, value, total) in enumerate(steps):
                laplace = total - 6.0 * value
                force = diffusion * laplace + reaction * value * (1.0 - value * value)
                integral = integral + own_weights[n] * force
                if n == 0:
                    own_laplace = laplace
                else:
                    own_value = jnp.where(node == n, value, own_value)
                    own_laplace = jnp.where(node == n, laplace, own_laplace)
            right[0, j, rows] = (integral - own_stiffness * own_laplace) * own_scale
            spare[0, j, rows] = (integral + (6.0 * own_stiffness) * own_value) * own_scale
    source, target = spare.at[0], spare.at[1]
    factor = own_stiffness * own_scale
    for level in range(JACOBI + 2, 2 * JACOBI):
        for start in chunks(level):
            rows = pl.ds(start, 8)
            for j, value, total in around(source, start, masks):
                target[j, rows] = right[0, j, rows] + factor * total
        source, target = target, source
    first_square = jnp.zeros((8, LANES), jnp.float32)
    second_square = jnp.zeros((8, LANES), jnp.float32)
    for start in chunks(2 * JACOBI):
        rows = pl.ds(start, 8)
        out_rows = pl.ds(start - PAD - HALO, 8)
        for j, value, total in around(source, start, masks):
            update = right[0, j, rows] + factor * total
            planes[j, out_rows] = update
            earlier = fields[node, j, rows]
            change = update - earlier
            second_square = second_square + change * change
            change = earlier - base[j, rows]
            first_square = first_square + change * change
    sums[0:1, :] = jnp.sum(first_square, axis=0, keepdims=True)
    sums[1:2, :] = jnp.sum(second_square, axis=0, keepdims=True)


def pairs_over(sizes, partner):
    pairs = []
    for index in np.ndindex(*sizes):
        other = partner(*[int(i) for i in index])
        if other is not None:
            pairs.append((int(np.ravel_multi_index(index, sizes)), int(np.ravel_multi_index(other, sizes))))
    return pairs


def shards(start_field, neighbours):
    nodes = lax.axis_size("node")
    axes = ("curve", "node", "sub")
    sizes = tuple(lax.axis_size(axis) for axis in axes)
    chips = sizes[0]
    weights, points = radau_tables(nodes)
    half = jax.ShapeDtypeStruct((EDGE, 8, LANES), jnp.float32)
    limit = pltpu.CompilerParams(vmem_limit_bytes=16 * 1024 * 1024)

    def across(curve, node, sub):
        if sub == 1 and curve + 1 < chips:
            return (curve + 1, node, 0)
        if sub == 0 and curve > 0:
            return (curve - 1, node, 1)
        return (curve, node ^ 1, sub) if node ^ 1 < nodes else None

    def beside(bit, swap):
        def partner(curve, node, sub):
            return (curve ^ bit, node, sub ^ swap)

        return partner

    def moved(value, partner):
        return lax.ppermute(value, axes, pairs_over(sizes, partner))

    chip_half, far_half = pl.pallas_call(
        split_kernel,
        out_shape=[half, half],
        in_specs=[VMEM, SMEM],
        out_specs=[VMEM, VMEM],
        compiler_params=limit,
    )(start_field, neighbours)
    far_got = moved(far_half, across)
    chip_got = moved(chip_half, beside(0, 1))
    planes, sums = pl.pallas_call(
        functools.partial(sweep_kernel, nodes, weights, points),
        out_shape=[
            jax.ShapeDtypeStruct((EDGE, EDGE, LANES), jnp.float32),
            jax.ShapeDtypeStruct((2, LANES), jnp.float32),
        ],
        in_specs=[VMEM] * 4,
        out_specs=[VMEM, VMEM],
        scratch_shapes=[
            pltpu.VMEM((EDGE, ROWS, LANES), jnp.float32),
            pltpu.VMEM((max(nodes, 2), EDGE, ROWS, LANES), jnp.float32),
            pltpu.VMEM((max(nodes, 2), EDGE, ROWS, LANES), jnp.float32),
            pltpu.VMEM((max(nodes, 2), EDGE, ROWS, LANES), jnp.float32),
        ],
        compiler_params=limit,
    )(chip_half, far_half, chip_got, far_got)
    field = pl.pallas_call(
        merge_kernel,
        out_shape=jax.ShapeDtypeStruct((1, 8, EDGE, EDGE * EDGE), jnp.float32),
        in_specs=[VMEM, SMEM],
        out_specs=VMEM,
        compiler_params=limit,
    )(planes, neighbours)
    sums = sums + moved(sums, beside(0, 1))
    bit = 1
    while bit < chips:
        sums = sums + moved(sums, beside(bit, 1))
        bit *= 2
    cells = start_field.size * chips * sizes[2]
    increments = jnp.sqrt(jnp.sum(sums, axis=1) / cells + 1e-06)
    return (field, increments[:, None])


def solution(mesh):
    placed = (P(("slab", "curve", "sub"), None, None), P(("slab", "curve", "sub"), None))
    return jax.shard_map(
        shards,
        mesh=mesh,
        in_specs=placed,
        out_specs=(P("node", ("slab", "curve", "sub"), None, None), P("slab", "node")),
        check_vma=False,
    )
```

```python
import functools

import jax
import jax.numpy as jnp
import numpy as np
from jax import lax
from jax.experimental import pallas as pl
from jax.experimental.pallas import tpu as pltpu
from jax.sharding import PartitionSpec as P

SWEEPS = 2
JACOBI = 4

diffusion = 0.5
reaction = 1.0
EDGE = 16
LANES = 128
CELLS = 16
SWAPS = ((4, 5), (2, 4), (1, 1), (8, 0))
VMEM = pl.BlockSpec(memory_space=pltpu.VMEM)


def legendre_value(order, place):
    before = 1.0
    current = place
    for degree in range(1, order):
        following = ((2 * degree + 1) * place * current - degree * before) / (degree + 1)
        before = current
        current = following
    return current


def radau_residue(node_count, moment):
    place = 2.0 * moment - 1.0
    return legendre_value(node_count, place) - legendre_value(node_count - 1, place)


def radau_tables(node_count):
    samples = 4000
    points = []
    for sample in range(samples - 1):
        left_end = sample / samples
        right_end = (sample + 1) / samples
        left_value = radau_residue(node_count, left_end)
        right_value = radau_residue(node_count, right_end)
        if left_value * right_value < 0.0:
            for halving in range(80):
                middle = 0.5 * (left_end + right_end)
                middle_value = radau_residue(node_count, middle)
                if left_value * middle_value <= 0.0:
                    right_end = middle
                else:
                    left_end = middle
                    left_value = middle_value
            points.append(0.5 * (left_end + right_end))
    points.append(1.0)
    table = []
    for row_node in range(node_count):
        table_row = []
        for col_node in range(node_count):
            factors = [1.0]
            for other_node in range(node_count):
                if other_node != col_node:
                    scale = 1.0 / (points[col_node] - points[other_node])
                    shifted = [0.0] + factors
                    product = [
                        shifted[place]
                        - points[other_node] * (factors[place] if place < len(factors) else 0.0)
                        for place in range(len(shifted))
                    ]
                    factors = [entry * scale for entry in product]
            integral = 0.0
            for power_index in range(len(factors)):
                integral = integral + factors[power_index] * points[row_node] ** (
                    power_index + 1
                ) / (power_index + 1)
            table_row.append(integral)
        table.append(table_row)
    return (np.array(table, dtype=np.float32), np.array(points, dtype=np.float32))


def swap_bits(values):
    lane = lax.broadcasted_iota(jnp.int32, (8, LANES), 1)
    for register_bit, lane_bit in SWAPS:
        shift = 1 << lane_bit
        high = (lane >> lane_bit) & 1 == 1
        out = list(values)
        for index in range(CELLS):
            if index & register_bit == 0:
                low_value, high_value = values[index], values[index | register_bit]
                out[index] = jnp.where(high, pltpu.roll(high_value, shift, 1), low_value)
                out[index | register_bit] = jnp.where(
                    high, high_value, pltpu.roll(low_value, LANES - shift, 1)
                )
        values = out
    return values


def cell_of(index):
    return ((index >> 1) & 3) * 4 + ((index & 1) << 1 | index >> 3)


def spread(source, store):
    values = [source[index & 7, :, (index >> 3) * LANES : (index >> 3) * LANES + LANES] for index in range(CELLS)]
    for index, value in enumerate(swap_bits(values)):
        store(cell_of(index), value)


def lane_of(slot, outer_j, outer_k):
    return (
        (outer_j & 1) << 6
        | (slot >> 2) << 5
        | ((slot >> 1) & 1) << 4
        | outer_k << 2
        | (slot & 1) << 1
        | outer_j >> 1
    )


def lane_routes(table, sub):
    lane = lax.broadcasted_iota(jnp.int32, (8, LANES), 1)
    row = lax.broadcasted_iota(jnp.int32, (8, LANES), 0)
    slot = ((lane >> 5) & 1) << 2 | ((lane >> 4) & 1) << 1 | (lane >> 1) & 1
    outer_j = (lane & 1) << 1 | lane >> 6
    outer_k = (lane >> 2) & 3
    named = []
    for face in range(6):
        column = jnp.broadcast_to(table[:, face : face + 1], (8, LANES))
        picked = jnp.sum(jnp.where(slot == row, column, 0), axis=0, keepdims=True)
        named.append(jnp.broadcast_to(picked, (8, LANES)))

    def inside(edge, face, within, wrapped):
        other = lane_of(named[face] & 7, *wrapped)
        other = jnp.where(named[face] < 0, LANES, other)
        return jnp.where(edge, other, lane_of(slot, *within))

    routes = [
        inside(outer_j == 0, 2, (outer_j - 1, outer_k), (3, outer_k)),
        inside(outer_j == 3, 3, (outer_j + 1, outer_k), (0, outer_k)),
        inside(outer_k == 0, 4, (outer_j, outer_k - 1), (outer_j, 3)),
        inside(outer_k == 3, 5, (outer_j, outer_k + 1), (outer_j, 0)),
    ]
    low = lane_of(named[0] & 7, outer_j, outer_k)
    high = lane_of(named[1] & 7, outer_j, outer_k)
    routes.append(jnp.where(sub == 0, high, low))
    routes.append(jnp.where(sub == 0, low, high))
    return routes


def picked(value, lanes):
    return jnp.take_along_axis(value, lanes, axis=1, mode="promise_in_bounds")


def halves_kernel(field, far_half, chip_half, far_done, chip_done):
    sub = lax.axis_index("sub")
    moves = []
    for target, start, done in (
        (far_half, sub * 8, far_done),
        (chip_half, 8 - sub * 8, chip_done),
    ):
        rows = pl.ds(pl.multiple_of(start, 8), 8)
        move = pltpu.make_async_copy(field.at[:, rows, :], target, done)
        move.start()
        moves.append(move)
    for move in moves:
        move.wait()


def merge_kernel(near, far, field):
    sub = lax.axis_index("sub")
    for planes, start in ((near, 8 - sub * 8), (far, sub * 8)):
        rows = pl.ds(pl.multiple_of(start, 8), 8)
        values = swap_bits([planes[cell_of(index)] for index in range(CELLS)])
        for index, value in enumerate(values):
            columns = slice((index >> 3) * LANES, (index >> 3) * LANES + LANES)
            field[0, index & 7, rows, columns] = value


def face_routes(routes):
    return [(route < LANES, route & (LANES - 1)) for route in routes[:4]]


def around(center, side_a, side_b, faces):
    def across(face, own, other):
        inner, lanes = faces[face]
        return jnp.where(inner, picked(other, lanes), own)

    cells = [center(cell) for cell in range(CELLS)]
    for cell in range(CELLS):
        value = cells[cell]
        inner_j, inner_k = cell // 4, cell % 4
        total = side_a(cell) + side_b(cell)
        below = cells[cell - 4] if inner_j > 0 else across(0, value, cells[cell + 12])
        above = cells[cell + 4] if inner_j < 3 else across(1, value, cells[cell - 12])
        before = cells[cell - 1] if inner_k > 0 else across(2, value, cells[cell + 3])
        behind = cells[cell + 1] if inner_k < 3 else across(3, value, cells[cell - 3])
        yield cell, value, (total + (below + above)) + (before + behind)


def around_at(source, start, step, faces):
    return around(
        lambda cell: source[cell, pl.ds(start, 8)],
        lambda cell: source[cell, pl.ds(start - step, 8)],
        lambda cell: source[cell, pl.ds(start + step, 8)],
        faces,
    )


class Scheme:
    def __init__(self, nodes, weights, points):
        one, six = np.float32(1.0), np.float32(6.0)
        self.nodes = nodes
        self.weights = weights
        self.stiffness = [np.float32(diffusion) * points[n] for n in range(nodes)]
        self.scales = [one / (one + six * a) for a in self.stiffness]
        self.whole = [np.float32(np.sum(weights[n].astype(np.float64))) for n in range(nodes)]
        self.count = 5 * nodes + 5

    def field(self, level, node=0):
        if level == 0:
            return 0
        if level <= JACOBI:
            return 1 + (level - 1) * self.nodes + node
        return JACOBI * self.nodes + level - JACOBI

    def right(self, sweep, node=0):
        return JACOBI * self.nodes + JACOBI + (node if sweep == 0 else self.nodes)

    def own(self, node, values):
        chosen = jnp.float32(values[0])
        for n in range(1, self.nodes):
            chosen = jnp.where(node == n, jnp.float32(values[n]), chosen)
        return chosen

    def first_step(self, value, total):
        laplace = total - 6.0 * value
        force = diffusion * laplace + reaction * value * (1.0 - value * value)
        for n in range(self.nodes):
            right = (value + self.whole[n] * force - self.stiffness[n] * laplace) * self.scales[n]
            yield n, right, value + (self.whole[n] * self.scales[n]) * force

    def second_step(self, node, start, steps):
        stiffness = self.own(node, self.stiffness)
        scale = self.own(node, self.scales)
        integral = start
        own_value, own_laplace = None, None
        for n, (_, value, total) in enumerate(steps):
            laplace = total - 6.0 * value
            force = diffusion * laplace + reaction * value * (1.0 - value * value)
            weight = self.own(node, [self.weights[m, n] for m in range(self.nodes)])
            integral = integral + weight * force
            own_value = value if n == 0 else jnp.where(node == n, value, own_value)
            own_laplace = laplace if n == 0 else jnp.where(node == n, laplace, own_laplace)
        right = (integral - stiffness * own_laplace) * scale
        return right, (integral + (6.0 * stiffness) * own_value) * scale

    def factor(self, node, sweep, n):
        if sweep == 0:
            return self.stiffness[n] * self.scales[n]
        return self.own(node, self.stiffness) * self.own(node, self.scales)


def near_kernel(scheme, chip_half, far_half, chip_got, table, edges, planes, sums, lanes, state):
    sub = lax.axis_index("sub")
    node = lax.axis_index("node")
    nodes = scheme.nodes
    routes = lane_routes(table, sub)
    for index, route in enumerate(routes):
        lanes[index] = route
    faces = face_routes(routes)
    low_half = pl.ds(pl.multiple_of(sub * 16, 8), 8)
    chip_half_rows = pl.ds(8, 8)
    high_half = pl.ds(pl.multiple_of(16 - sub * 16, 8), 8)

    def store_far(cell, value):
        state[0, cell, low_half] = value
        edges[0, 0, cell] = value
        edges[1, 0, cell] = value

    def store_chip(cell, value):
        state[0, cell, chip_half_rows] = value

    def store_got(cell, value):
        state[0, cell, high_half] = picked(value, routes[4])

    spread(far_half, store_far)
    spread(chip_half, store_chip)
    spread(chip_got, store_got)

    span = EDGE + 8

    def starts(level):
        count = -(-(span - 2 * level) // 8)
        if count == 1:
            return [level]
        return [level + round(piece * (span - 2 * level - 8) / (count - 1)) for piece in range(count)]

    def keep(index, level, start, cell, value):
        state[index, cell, pl.ds(start, 8)] = value
        if start == level:
            edges[0, index, cell] = value
        if start == span - 8 - level:
            edges[1, index, cell] = value

    for start in starts(1):
        for cell, value, total in around_at(state.at[0], start, 1, faces):
            for n, right, update in scheme.first_step(value, total):
                keep(scheme.right(0, n), 1, start, cell, right)
                keep(scheme.field(1, n), 1, start, cell, update)
    for level in range(2, JACOBI + 1):
        for start in starts(level):
            for n in range(nodes):
                factor = scheme.factor(node, 0, n)
                for cell, value, total in around_at(state.at[scheme.field(level - 1, n)], start, 1, faces):
                    right = state[scheme.right(0, n), cell, pl.ds(start, 8)]
                    keep(scheme.field(level, n), level, start, cell, right + factor * total)
    level = JACOBI + 1
    for start in starts(level):
        sources = [state.at[scheme.field(JACOBI, n)] for n in range(nodes)]
        for steps in zip(*[around_at(source, start, 1, faces) for source in sources]):
            cell = steps[0][0]
            right, update = scheme.second_step(node, state[0, cell, pl.ds(start, 8)], steps)
            keep(scheme.right(1), level, start, cell, right)
            keep(scheme.field(level), level, start, cell, update)
    factor = scheme.factor(node, 1, 0)
    for level in range(JACOBI + 2, 2 * JACOBI):
        for start in starts(level):
            for cell, value, total in around_at(state.at[scheme.field(level - 1)], start, 1, faces):
                right = state[scheme.right(1), cell, pl.ds(start, 8)]
                keep(scheme.field(level), level, start, cell, right + factor * total)
    first_square = jnp.zeros((8, LANES), jnp.float32)
    second_square = jnp.zeros((8, LANES), jnp.float32)
    start = 2 * JACOBI
    rows = pl.ds(start, 8)
    earlier_place = scheme.field(JACOBI) + node
    for cell, value, total in around_at(state.at[scheme.field(start - 1)], start, 1, faces):
        update = state[scheme.right(1), cell, rows] + factor * total
        planes[cell] = update
        earlier = state[earlier_place, cell, rows]
        change = update - earlier
        second_square = second_square + change * change
        change = earlier - state[0, cell, rows]
        first_square = first_square + change * change
    sums[0] = first_square
    sums[1] = second_square


def far_kernel(scheme, far_got, edges, near_sums, lanes, planes, sums, state):
    sub = lax.axis_index("sub")
    curve = lax.axis_index("curve")
    node = lax.axis_index("node")
    nodes = scheme.nodes
    faces = face_routes([lanes[index] for index in range(4)])
    toward = 1 - 2 * sub
    at_end = jnp.where(sub == 0, curve == 0, curve == lax.axis_size("curve") - 1)
    beside = pl.ds(pl.multiple_of(8 + 8 * toward, 8), 8)
    new = pl.ds(8, 8)
    for index in range(scheme.count):
        for cell in range(CELLS):
            state[index, cell, beside] = edges[sub, index, cell]

    def store_far(cell, value):
        state[0, cell, new] = picked(value, lanes[5])

    spread(far_got, store_far)

    @pl.when(at_end)
    def _():
        for row in range(8):
            state[0, :, 15 - row : 16 - row, :] = edges[sub, 0, :, row : row + 1, :]

    def shifted(levels):
        return pl.ds(8 + toward * levels, 8)

    def ring(index):
        source = state.at[index]
        return around(
            lambda cell: source[cell, shifted(1)],
            lambda cell: source[cell, new],
            lambda cell: source[cell, shifted(2)],
            faces,
        )

    def write(pending):
        for index, cell, value in pending:
            state[index, cell, new] = value

    pending = []
    for cell, value, total in ring(0):
        for n, right, update in scheme.first_step(value, total):
            pending.append((scheme.right(0, n), cell, right))
            pending.append((scheme.field(1, n), cell, update))
    write(pending)
    for level in range(2, JACOBI + 1):
        pending = []
        for n in range(nodes):
            factor = scheme.factor(node, 0, n)
            for cell, value, total in ring(scheme.field(level - 1, n)):
                right = state[scheme.right(0, n), cell, shifted(level - 1)]
                pending.append((scheme.field(level, n), cell, right + factor * total))
        write(pending)
    level = JACOBI + 1
    pending = []
    for steps in zip(*[ring(scheme.field(JACOBI, n)) for n in range(nodes)]):
        cell = steps[0][0]
        right, update = scheme.second_step(node, state[0, cell, shifted(level)], steps)
        pending.append((scheme.right(1), cell, right))
        pending.append((scheme.field(level), cell, update))
    write(pending)
    factor = scheme.factor(node, 1, 0)
    for level in range(JACOBI + 2, 2 * JACOBI):
        pending = []
        for cell, value, total in ring(scheme.field(level - 1)):
            right = state[scheme.right(1), cell, shifted(level - JACOBI - 1)]
            pending.append((scheme.field(level), cell, right + factor * total))
        write(pending)
    first_square = near_sums[0]
    second_square = near_sums[1]
    level = 2 * JACOBI
    for cell, value, total in ring(scheme.field(level - 1)):
        update = state[scheme.right(1), cell, shifted(JACOBI - 1)] + factor * total
        planes[cell] = update
        earlier = state[scheme.field(JACOBI) + node, cell, shifted(JACOBI)]
        change = update - earlier
        second_square = second_square + change * change
        change = earlier - state[0, cell, shifted(level)]
        first_square = first_square + change * change
    sums[0:1, :] = jnp.sum(first_square, axis=0, keepdims=True)
    sums[1:2, :] = jnp.sum(second_square, axis=0, keepdims=True)


def pairs_over(sizes, partner):
    pairs = []
    for index in np.ndindex(*sizes):
        other = partner(*[int(i) for i in index])
        if other is not None:
            pairs.append((int(np.ravel_multi_index(index, sizes)), int(np.ravel_multi_index(other, sizes))))
    return pairs


def shards(start_field, neighbours):
    nodes = lax.axis_size("node")
    axes = ("curve", "node", "sub")
    sizes = tuple(lax.axis_size(axis) for axis in axes)
    chips = sizes[0]
    scheme = Scheme(nodes, *radau_tables(nodes))
    half = jax.ShapeDtypeStruct((8, 8, EDGE * EDGE), jnp.float32)
    planes = jax.ShapeDtypeStruct((CELLS, 8, LANES), jnp.float32)
    limit = pltpu.CompilerParams(vmem_limit_bytes=24 * 1024 * 1024)

    def across(curve, node, sub):
        if sub == 1 and curve + 1 < chips:
            return (curve + 1, node, 0)
        if sub == 0 and curve > 0:
            return (curve - 1, node, 1)
        return (curve, node ^ 1, sub) if node ^ 1 < nodes else None

    def beside(bit, swap):
        def partner(curve, node, sub):
            return (curve ^ bit, node, sub ^ swap)

        return partner

    def moved(value, partner):
        return lax.ppermute(value, axes, pairs_over(sizes, partner))

    far_half, chip_half = pl.pallas_call(
        halves_kernel,
        out_shape=[half, half],
        in_specs=[pl.BlockSpec(memory_space=pltpu.HBM)],
        out_specs=[VMEM, VMEM],
        scratch_shapes=[pltpu.SemaphoreType.DMA, pltpu.SemaphoreType.DMA],
        compiler_params=limit,
    )(start_field)
    far_got = moved(far_half, across)
    chip_got = moved(chip_half, beside(0, 1))
    edges, near_planes, near_sums, lanes = pl.pallas_call(
        functools.partial(near_kernel, scheme),
        out_shape=[
            jax.ShapeDtypeStruct((2, scheme.count, CELLS, 8, LANES), jnp.float32),
            planes,
            jax.ShapeDtypeStruct((2, 8, LANES), jnp.float32),
            jax.ShapeDtypeStruct((6, 8, LANES), jnp.int32),
        ],
        in_specs=[VMEM] * 4,
        out_specs=[VMEM] * 4,
        scratch_shapes=[pltpu.VMEM((scheme.count, CELLS, EDGE + 8, LANES), jnp.float32)],
        compiler_params=limit,
        cost_estimate=pl.CostEstimate(flops=8_000_000, bytes_accessed=2_000_000, transcendentals=0),
    )(chip_half, far_half, chip_got, neighbours)
    far_planes, sums = pl.pallas_call(
        functools.partial(far_kernel, scheme),
        out_shape=[planes, jax.ShapeDtypeStruct((2, LANES), jnp.float32)],
        in_specs=[VMEM] * 4,
        out_specs=[VMEM, VMEM],
        scratch_shapes=[pltpu.VMEM((scheme.count, CELLS, EDGE + 8, LANES), jnp.float32)],
        compiler_params=limit,
    )(far_got, edges, near_sums, lanes)
    field = pl.pallas_call(
        merge_kernel,
        out_shape=jax.ShapeDtypeStruct((1, 8, EDGE, EDGE * EDGE), jnp.float32),
        in_specs=[VMEM, VMEM],
        out_specs=VMEM,
        compiler_params=limit,
    )(near_planes, far_planes)
    sums = sums + moved(sums, beside(0, 1))
    bit = 1
    while bit < chips:
        sums = sums + moved(sums, beside(bit, 1))
        bit *= 2
    cells = start_field.size * chips * sizes[2]
    increments = jnp.sqrt(jnp.sum(sums, axis=1) / cells + 1e-06)
    return (field, increments[:, None])


def solution(mesh):
    placed = (P(("slab", "curve", "sub"), None, None), P(("slab", "curve", "sub"), None))
    return jax.shard_map(
        shards,
        mesh=mesh,
        in_specs=placed,
        out_specs=(P("node", ("slab", "curve", "sub"), None, None), P("slab", "node")),
        check_vma=False,
    )
```

```python
import functools

import jax
import jax.numpy as jnp
import numpy as np
from jax import lax
from jax.experimental import pallas as pl
from jax.experimental.pallas import tpu as pltpu
from jax.sharding import PartitionSpec as P

SWEEPS = 2
JACOBI = 4

diffusion = 0.5
reaction = 1.0
EDGE = 16
LANES = 128
CELLS = 16
SWAPS = ((4, 5), (2, 4), (1, 1), (8, 0))
VMEM = pl.BlockSpec(memory_space=pltpu.VMEM)


def legendre_value(order, place):
    before = 1.0
    current = place
    for degree in range(1, order):
        following = ((2 * degree + 1) * place * current - degree * before) / (degree + 1)
        before = current
        current = following
    return current


def radau_residue(node_count, moment):
    place = 2.0 * moment - 1.0
    return legendre_value(node_count, place) - legendre_value(node_count - 1, place)


def radau_tables(node_count):
    samples = 4000
    points = []
    for sample in range(samples - 1):
        left_end = sample / samples
        right_end = (sample + 1) / samples
        left_value = radau_residue(node_count, left_end)
        right_value = radau_residue(node_count, right_end)
        if left_value * right_value < 0.0:
            for halving in range(80):
                middle = 0.5 * (left_end + right_end)
                middle_value = radau_residue(node_count, middle)
                if left_value * middle_value <= 0.0:
                    right_end = middle
                else:
                    left_end = middle
                    left_value = middle_value
            points.append(0.5 * (left_end + right_end))
    points.append(1.0)
    table = []
    for row_node in range(node_count):
        table_row = []
        for col_node in range(node_count):
            factors = [1.0]
            for other_node in range(node_count):
                if other_node != col_node:
                    scale = 1.0 / (points[col_node] - points[other_node])
                    shifted = [0.0] + factors
                    product = [
                        shifted[place]
                        - points[other_node] * (factors[place] if place < len(factors) else 0.0)
                        for place in range(len(shifted))
                    ]
                    factors = [entry * scale for entry in product]
            integral = 0.0
            for power_index in range(len(factors)):
                integral = integral + factors[power_index] * points[row_node] ** (
                    power_index + 1
                ) / (power_index + 1)
            table_row.append(integral)
        table.append(table_row)
    return (np.array(table, dtype=np.float32), np.array(points, dtype=np.float32))


def swap_bits(values):
    lane = lax.broadcasted_iota(jnp.int32, (8, LANES), 1)
    for register_bit, lane_bit in SWAPS:
        shift = 1 << lane_bit
        high = (lane >> lane_bit) & 1 == 1
        out = list(values)
        for index in range(CELLS):
            if index & register_bit == 0:
                low_value, high_value = values[index], values[index | register_bit]
                out[index] = jnp.where(high, pltpu.roll(high_value, shift, 1), low_value)
                out[index | register_bit] = jnp.where(
                    high, high_value, pltpu.roll(low_value, LANES - shift, 1)
                )
        values = out
    return values


def cell_of(index):
    return ((index >> 1) & 3) * 4 + ((index & 1) << 1 | index >> 3)


def spread(source, store):
    values = [source[index & 7, :, (index >> 3) * LANES : (index >> 3) * LANES + LANES] for index in range(CELLS)]
    for index, value in enumerate(swap_bits(values)):
        store(cell_of(index), value)


def spread_to(source, route, store):
    lane = lax.broadcasted_iota(jnp.int32, (8, LANES), 1)
    values = [source[index & 7, :, (index >> 3) * LANES : (index >> 3) * LANES + LANES] for index in range(CELLS)]
    for stage, origin in ((0, None), (2, route)):
        (bit_a, lane_a), (bit_b, lane_b) = SWAPS[stage : stage + 2]
        spot = lane if origin is None else origin
        high_a = (spot >> lane_a) & 1 == 1
        high_b = (spot >> lane_b) & 1 == 1
        shifts = {}

        def moved_by(value, step_a, step_b):
            shift = step_a * (1 << lane_a) + step_b * (1 << lane_b)
            if origin is None:
                return value if shift == 0 else pltpu.roll(value, -shift % LANES, 1)
            if shift not in shifts:
                shifts[shift] = (origin + shift) & (LANES - 1)
            return picked(value, shifts[shift])

        out = []
        for index in range(CELLS):
            base = index & ~(bit_a | bit_b)
            own_a, own_b = int(index & bit_a != 0), int(index & bit_b != 0)
            parts = [
                [moved_by(values[base | p * bit_a | q * bit_b], own_a - p, own_b - q) for q in range(2)]
                for p in range(2)
            ]
            rows = [jnp.where(high_b, part[1], part[0]) for part in parts]
            out.append(jnp.where(high_a, rows[1], rows[0]))
        values = out
    for index, value in enumerate(values):
        store(cell_of(index), value)


def lane_of(slot, outer_j, outer_k):
    return (
        (outer_j & 1) << 6
        | (slot >> 2) << 5
        | ((slot >> 1) & 1) << 4
        | outer_k << 2
        | (slot & 1) << 1
        | outer_j >> 1
    )


def lane_routes(table, sub):
    lane = lax.broadcasted_iota(jnp.int32, (8, LANES), 1)
    row = lax.broadcasted_iota(jnp.int32, (8, LANES), 0)
    slot = ((lane >> 5) & 1) << 2 | ((lane >> 4) & 1) << 1 | (lane >> 1) & 1
    outer_j = (lane & 1) << 1 | lane >> 6
    outer_k = (lane >> 2) & 3
    named = []
    for face in range(6):
        column = jnp.broadcast_to(table[:, face : face + 1], (8, LANES))
        picked = jnp.sum(jnp.where(slot == row, column, 0), axis=0, keepdims=True)
        named.append(jnp.broadcast_to(picked, (8, LANES)))

    def inside(edge, face, within, wrapped):
        other = lane_of(named[face] & 7, *wrapped)
        other = jnp.where(named[face] < 0, LANES, other)
        return jnp.where(edge, other, lane_of(slot, *within))

    routes = [
        inside(outer_j == 0, 2, (outer_j - 1, outer_k), (3, outer_k)),
        inside(outer_j == 3, 3, (outer_j + 1, outer_k), (0, outer_k)),
        inside(outer_k == 0, 4, (outer_j, outer_k - 1), (outer_j, 3)),
        inside(outer_k == 3, 5, (outer_j, outer_k + 1), (outer_j, 0)),
    ]
    low = lane_of(named[0] & 7, outer_j, outer_k)
    high = lane_of(named[1] & 7, outer_j, outer_k)
    routes.append(jnp.where(sub == 0, high, low))
    routes.append(jnp.where(sub == 0, low, high))
    return routes


def picked(value, lanes):
    return jnp.take_along_axis(value, lanes, axis=1, mode="promise_in_bounds")


def halves_kernel(field, far_half, chip_half, far_done, chip_done):
    sub = lax.axis_index("sub")
    moves = []
    for target, start, done in (
        (far_half, sub * 8, far_done),
        (chip_half, 8 - sub * 8, chip_done),
    ):
        rows = pl.ds(pl.multiple_of(start, 8), 8)
        move = pltpu.make_async_copy(field.at[:, rows, :], target, done)
        move.start()
        moves.append(move)
    for move in moves:
        move.wait()


def merge_kernel(near, far, field):
    sub = lax.axis_index("sub")
    for planes, start in ((near, 8 - sub * 8), (far, sub * 8)):
        rows = pl.ds(pl.multiple_of(start, 8), 8)
        values = swap_bits([planes[cell_of(index)] for index in range(CELLS)])
        for index, value in enumerate(values):
            columns = slice((index >> 3) * LANES, (index >> 3) * LANES + LANES)
            field[0, index & 7, rows, columns] = value


def face_routes(routes):
    return [(route < LANES, route & (LANES - 1)) for route in routes[:4]]


def around(center, side_a, side_b, faces):
    def across(face, own, other):
        inner, lanes = faces[face]
        return jnp.where(inner, picked(other, lanes), own)

    cells = [center(cell) for cell in range(CELLS)]
    for cell in range(CELLS):
        value = cells[cell]
        inner_j, inner_k = cell // 4, cell % 4
        total = side_a(cell) + side_b(cell)
        below = cells[cell - 4] if inner_j > 0 else across(0, value, cells[cell + 12])
        above = cells[cell + 4] if inner_j < 3 else across(1, value, cells[cell - 12])
        before = cells[cell - 1] if inner_k > 0 else across(2, value, cells[cell + 3])
        behind = cells[cell + 1] if inner_k < 3 else across(3, value, cells[cell - 3])
        yield cell, value, (total + (below + above)) + (before + behind)


def around_at(source, start, step, faces):
    return around(
        lambda cell: source[cell, pl.ds(start, 8)],
        lambda cell: source[cell, pl.ds(start - step, 8)],
        lambda cell: source[cell, pl.ds(start + step, 8)],
        faces,
    )


class Scheme:
    def __init__(self, nodes, weights, points):
        one, six = np.float32(1.0), np.float32(6.0)
        self.nodes = nodes
        self.weights = weights
        self.stiffness = [np.float32(diffusion) * points[n] for n in range(nodes)]
        self.scales = [one / (one + six * a) for a in self.stiffness]
        self.whole = [np.float32(np.sum(weights[n].astype(np.float64))) for n in range(nodes)]
        self.count = 5 * nodes + 5

    def field(self, level, node=0):
        if level == 0:
            return 0
        if level <= JACOBI:
            return 1 + (level - 1) * self.nodes + node
        return JACOBI * self.nodes + level - JACOBI

    def right(self, sweep, node=0):
        return JACOBI * self.nodes + JACOBI + (node if sweep == 0 else self.nodes)

    def own(self, node, values):
        chosen = jnp.float32(values[0])
        for n in range(1, self.nodes):
            chosen = jnp.where(node == n, jnp.float32(values[n]), chosen)
        return chosen

    def first_step(self, value, total):
        laplace = total - 6.0 * value
        force = diffusion * laplace + reaction * value * (1.0 - value * value)
        for n in range(self.nodes):
            right = (value + self.whole[n] * force - self.stiffness[n] * laplace) * self.scales[n]
            yield n, right, value + (self.whole[n] * self.scales[n]) * force

    def second_step(self, node, start, steps):
        stiffness = self.own(node, self.stiffness)
        scale = self.own(node, self.scales)
        integral = start
        own_value, own_laplace = None, None
        for n, (_, value, total) in enumerate(steps):
            laplace = total - 6.0 * value
            force = diffusion * laplace + reaction * value * (1.0 - value * value)
            weight = self.own(node, [self.weights[m, n] for m in range(self.nodes)])
            integral = integral + weight * force
            own_value = value if n == 0 else jnp.where(node == n, value, own_value)
            own_laplace = laplace if n == 0 else jnp.where(node == n, laplace, own_laplace)
        right = (integral - stiffness * own_laplace) * scale
        return right, (integral + (6.0 * stiffness) * own_value) * scale

    def factor(self, node, sweep, n):
        if sweep == 0:
            return self.stiffness[n] * self.scales[n]
        return self.own(node, self.stiffness) * self.own(node, self.scales)


def near_kernel(scheme, chip_half, far_half, chip_got, table, edges, mirror, planes, sums, lanes, state):
    sub = lax.axis_index("sub")
    node = lax.axis_index("node")
    nodes = scheme.nodes
    routes = lane_routes(table, sub)
    for index, route in enumerate(routes):
        lanes[index] = route
    faces = face_routes(routes)
    below, above = slice(0, 8), slice(16, 24)
    low_half = pl.ds(pl.multiple_of(sub * 16, 8), 8)
    chip_half_rows = pl.ds(8, 8)
    high_half = pl.ds(pl.multiple_of(16 - sub * 16, 8), 8)

    def store_far(cell, value):
        state[0, cell, low_half] = value
        edges[0, cell, above] = value
        edges[0, cell, below] = value

    def store_chip(cell, value):
        state[0, cell, chip_half_rows] = value

    def store_got(cell, value):
        state[0, cell, high_half] = picked(value, routes[4])

    spread(far_half, store_far)
    spread(chip_half, store_chip)
    spread(chip_got, store_got)
    for row in range(8):
        mirror[:, 7 - row : 8 - row, :] = edges[0, :, row : row + 1, :]

    span = EDGE + 8

    def starts(level):
        count = -(-(span - 2 * level) // 8)
        if count == 1:
            return [level]
        return [level + round(piece * (span - 2 * level - 8) / (count - 1)) for piece in range(count)]

    def keep(index, level, start, cell, value):
        state[index, cell, pl.ds(start, 8)] = value
        if start == level:
            edges[index, cell, above] = value
        if start == span - 8 - level:
            edges[index, cell, below] = value

    for start in starts(1):
        for cell, value, total in around_at(state.at[0], start, 1, faces):
            for n, right, update in scheme.first_step(value, total):
                keep(scheme.right(0, n), 1, start, cell, right)
                keep(scheme.field(1, n), 1, start, cell, update)
    for level in range(2, JACOBI + 1):
        for start in starts(level):
            for n in range(nodes):
                factor = scheme.factor(node, 0, n)
                for cell, value, total in around_at(state.at[scheme.field(level - 1, n)], start, 1, faces):
                    right = state[scheme.right(0, n), cell, pl.ds(start, 8)]
                    keep(scheme.field(level, n), level, start, cell, right + factor * total)
    level = JACOBI + 1
    for start in starts(level):
        sources = [state.at[scheme.field(JACOBI, n)] for n in range(nodes)]
        for steps in zip(*[around_at(source, start, 1, faces) for source in sources]):
            cell = steps[0][0]
            right, update = scheme.second_step(node, state[0, cell, pl.ds(start, 8)], steps)
            keep(scheme.right(1), level, start, cell, right)
            keep(scheme.field(level), level, start, cell, update)
    factor = scheme.factor(node, 1, 0)
    for level in range(JACOBI + 2, 2 * JACOBI):
        for start in starts(level):
            for cell, value, total in around_at(state.at[scheme.field(level - 1)], start, 1, faces):
                right = state[scheme.right(1), cell, pl.ds(start, 8)]
                keep(scheme.field(level), level, start, cell, right + factor * total)
    first_square = jnp.zeros((8, LANES), jnp.float32)
    second_square = jnp.zeros((8, LANES), jnp.float32)
    start = 2 * JACOBI
    rows = pl.ds(start, 8)
    earlier_place = scheme.field(JACOBI) + node
    for cell, value, total in around_at(state.at[scheme.field(start - 1)], start, 1, faces):
        update = state[scheme.right(1), cell, rows] + factor * total
        planes[cell] = update
        earlier = state[earlier_place, cell, rows]
        change = update - earlier
        second_square = second_square + change * change
        change = earlier - state[0, cell, rows]
        first_square = first_square + change * change
    sums[0] = first_square
    sums[1] = second_square


def far_kernel(scheme, far_got, edges, mirror, near_sums, lanes, planes, sums, state):
    sub = lax.axis_index("sub")
    for side in range(2):

        @pl.when(sub == side)
        def _():
            far_side(scheme, side, far_got, mirror, near_sums, lanes, planes, sums, state)


def far_side(scheme, side, far_got, mirror, near_sums, lanes, planes, sums, state):
    curve = lax.axis_index("curve")
    node = lax.axis_index("node")
    nodes = scheme.nodes
    faces = face_routes([lanes[index] for index in range(4)])
    toward = 1 - 2 * side
    at_end = curve == (0 if side == 0 else lax.axis_size("curve") - 1)
    new = pl.ds(8, 8)

    def store_far(cell, value):
        state[0, cell, new] = jnp.where(at_end, mirror[cell], value)

    spread_to(far_got, lanes[5], store_far)

    def shifted(levels):
        return pl.ds(8 + toward * levels, 8)

    def ring(index):
        source = state.at[index]
        return around(
            lambda cell: source[cell, shifted(1)],
            lambda cell: source[cell, new],
            lambda cell: source[cell, shifted(2)],
            faces,
        )

    def write(pending):
        for index, cell, value in pending:
            state[index, cell, new] = value

    pending = []
    for cell, value, total in ring(0):
        for n, right, update in scheme.first_step(value, total):
            pending.append((scheme.right(0, n), cell, right))
            pending.append((scheme.field(1, n), cell, update))
    write(pending)
    for level in range(2, JACOBI + 1):
        pending = []
        for n in range(nodes):
            factor = scheme.factor(node, 0, n)
            for cell, value, total in ring(scheme.field(level - 1, n)):
                right = state[scheme.right(0, n), cell, shifted(level - 1)]
                pending.append((scheme.field(level, n), cell, right + factor * total))
        write(pending)
    level = JACOBI + 1
    pending = []
    for steps in zip(*[ring(scheme.field(JACOBI, n)) for n in range(nodes)]):
        cell = steps[0][0]
        right, update = scheme.second_step(node, state[0, cell, shifted(level)], steps)
        pending.append((scheme.right(1), cell, right))
        pending.append((scheme.field(level), cell, update))
    write(pending)
    factor = scheme.factor(node, 1, 0)
    for level in range(JACOBI + 2, 2 * JACOBI):
        pending = []
        for cell, value, total in ring(scheme.field(level - 1)):
            right = state[scheme.right(1), cell, shifted(level - JACOBI - 1)]
            pending.append((scheme.field(level), cell, right + factor * total))
        write(pending)
    level = 2 * JACOBI
    first_squares, second_squares = [near_sums[0]], [near_sums[1]]
    for cell, value, total in ring(scheme.field(level - 1)):
        update = state[scheme.right(1), cell, shifted(JACOBI - 1)] + factor * total
        planes[cell] = update
        earlier = state[scheme.field(JACOBI) + node, cell, shifted(JACOBI)]
        change = update - earlier
        second_squares.append(change * change)
        change = earlier - state[0, cell, shifted(level)]
        first_squares.append(change * change)
    sums[0] = added(first_squares)
    sums[1] = added(second_squares)


def added(terms):
    while len(terms) > 1:
        terms = [sum(terms[place + 1 : place + 2], terms[place]) for place in range(0, len(terms), 2)]
    return terms[0]


def pairs_over(sizes, partner):
    pairs = []
    for index in np.ndindex(*sizes):
        other = partner(*[int(i) for i in index])
        if other is not None:
            pairs.append((int(np.ravel_multi_index(index, sizes)), int(np.ravel_multi_index(other, sizes))))
    return pairs


def shards(start_field, neighbours):
    nodes = lax.axis_size("node")
    axes = ("curve", "node", "sub")
    sizes = tuple(lax.axis_size(axis) for axis in axes)
    chips = sizes[0]
    scheme = Scheme(nodes, *radau_tables(nodes))
    half = jax.ShapeDtypeStruct((8, 8, EDGE * EDGE), jnp.float32)
    planes = jax.ShapeDtypeStruct((CELLS, 8, LANES), jnp.float32)
    limit = pltpu.CompilerParams(vmem_limit_bytes=24 * 1024 * 1024)

    def across(curve, node, sub):
        if sub == 1 and curve + 1 < chips:
            return (curve + 1, node, 0)
        if sub == 0 and curve > 0:
            return (curve - 1, node, 1)
        return (curve, node ^ 1, sub) if node ^ 1 < nodes else None

    def beside(bit, swap):
        def partner(curve, node, sub):
            return (curve ^ bit, node, sub ^ swap)

        return partner

    def moved(value, partner):
        return lax.ppermute(value, axes, pairs_over(sizes, partner))

    far_half, chip_half = pl.pallas_call(
        halves_kernel,
        out_shape=[half, half],
        in_specs=[pl.BlockSpec(memory_space=pltpu.HBM)],
        out_specs=[VMEM, VMEM],
        scratch_shapes=[pltpu.SemaphoreType.DMA, pltpu.SemaphoreType.DMA],
        compiler_params=limit,
    )(start_field)
    far_got = moved(far_half, across)
    chip_got = moved(chip_half, beside(0, 1))
    shared = jax.ShapeDtypeStruct((scheme.count, CELLS, EDGE + 8, LANES), jnp.float32)
    edges, mirror, near_planes, near_sums, lanes = pl.pallas_call(
        functools.partial(near_kernel, scheme),
        out_shape=[
            shared,
            planes,
            planes,
            jax.ShapeDtypeStruct((2, 8, LANES), jnp.float32),
            jax.ShapeDtypeStruct((6, 8, LANES), jnp.int32),
        ],
        in_specs=[VMEM] * 4,
        out_specs=[VMEM] * 5,
        scratch_shapes=[pltpu.VMEM(shared.shape, jnp.float32)],
        compiler_params=limit,
        cost_estimate=pl.CostEstimate(flops=8_000_000, bytes_accessed=2_000_000, transcendentals=0),
    )(chip_half, far_half, chip_got, neighbours)
    far_planes, sums, _ = pl.pallas_call(
        functools.partial(far_kernel, scheme),
        out_shape=[planes, jax.ShapeDtypeStruct((2, 8, LANES), jnp.float32), shared],
        in_specs=[VMEM] * 5,
        out_specs=[VMEM] * 3,
        input_output_aliases={1: 2},
        compiler_params=limit,
    )(far_got, edges, mirror, near_sums, lanes)
    field = pl.pallas_call(
        merge_kernel,
        out_shape=jax.ShapeDtypeStruct((1, 8, EDGE, EDGE * EDGE), jnp.float32),
        in_specs=[VMEM, VMEM],
        out_specs=VMEM,
        compiler_params=limit,
    )(near_planes, far_planes)
    sums = sums + moved(sums, beside(0, 1))
    bit = 1
    while bit < chips:
        sums = sums + moved(sums, beside(bit, 1))
        bit *= 2
    cells = start_field.size * chips * sizes[2]
    increments = jnp.sqrt(jnp.sum(sums, axis=(1, 2)) / cells + 1e-06)
    return (field, increments[:, None])


def solution(mesh):
    placed = (P(("slab", "curve", "sub"), None, None), P(("slab", "curve", "sub"), None))
    return jax.shard_map(
        shards,
        mesh=mesh,
        in_specs=placed,
        out_specs=(P("node", ("slab", "curve", "sub"), None, None), P("slab", "node")),
        check_vma=False,
    )
```

```python
import functools

import jax
import jax.numpy as jnp
import numpy as np
from jax import lax
from jax.experimental import pallas as pl
from jax.experimental.pallas import tpu as pltpu
from jax.sharding import PartitionSpec as P

SWEEPS = 2
JACOBI = 4

diffusion = 0.5
reaction = 1.0
EDGE = 16
LANES = 128
CELLS = 16
SWAPS = ((4, 5), (2, 4), (1, 1), (8, 0))
VMEM = pl.BlockSpec(memory_space=pltpu.VMEM)


def legendre_value(order, place):
    before = 1.0
    current = place
    for degree in range(1, order):
        following = ((2 * degree + 1) * place * current - degree * before) / (degree + 1)
        before = current
        current = following
    return current


def radau_residue(node_count, moment):
    place = 2.0 * moment - 1.0
    return legendre_value(node_count, place) - legendre_value(node_count - 1, place)


def radau_tables(node_count):
    samples = 4000
    points = []
    for sample in range(samples - 1):
        left_end = sample / samples
        right_end = (sample + 1) / samples
        left_value = radau_residue(node_count, left_end)
        right_value = radau_residue(node_count, right_end)
        if left_value * right_value < 0.0:
            for halving in range(80):
                middle = 0.5 * (left_end + right_end)
                middle_value = radau_residue(node_count, middle)
                if left_value * middle_value <= 0.0:
                    right_end = middle
                else:
                    left_end = middle
                    left_value = middle_value
            points.append(0.5 * (left_end + right_end))
    points.append(1.0)
    table = []
    for row_node in range(node_count):
        table_row = []
        for col_node in range(node_count):
            factors = [1.0]
            for other_node in range(node_count):
                if other_node != col_node:
                    scale = 1.0 / (points[col_node] - points[other_node])
                    shifted = [0.0] + factors
                    product = [
                        shifted[place]
                        - points[other_node] * (factors[place] if place < len(factors) else 0.0)
                        for place in range(len(shifted))
                    ]
                    factors = [entry * scale for entry in product]
            integral = 0.0
            for power_index in range(len(factors)):
                integral = integral + factors[power_index] * points[row_node] ** (
                    power_index + 1
                ) / (power_index + 1)
            table_row.append(integral)
        table.append(table_row)
    return (np.array(table, dtype=np.float32), np.array(points, dtype=np.float32))


def swap_bits(values):
    lane = lax.broadcasted_iota(jnp.int32, (8, LANES), 1)
    for register_bit, lane_bit in SWAPS:
        shift = 1 << lane_bit
        high = (lane >> lane_bit) & 1 == 1
        out = list(values)
        for index in range(CELLS):
            if index & register_bit == 0:
                low_value, high_value = values[index], values[index | register_bit]
                out[index] = jnp.where(high, pltpu.roll(high_value, shift, 1), low_value)
                out[index | register_bit] = jnp.where(
                    high, high_value, pltpu.roll(low_value, LANES - shift, 1)
                )
        values = out
    return values


def cell_of(index):
    return ((index >> 1) & 3) * 4 + ((index & 1) << 1 | index >> 3)


def spread(source, store):
    values = [source[index & 7, :, (index >> 3) * LANES : (index >> 3) * LANES + LANES] for index in range(CELLS)]
    for index, value in enumerate(swap_bits(values)):
        store(cell_of(index), value)


def spread_to(source, route, store):
    lane = lax.broadcasted_iota(jnp.int32, (8, LANES), 1)
    values = [source[index & 7, :, (index >> 3) * LANES : (index >> 3) * LANES + LANES] for index in range(CELLS)]
    for stage, origin in ((0, None), (2, route)):
        (bit_a, lane_a), (bit_b, lane_b) = SWAPS[stage : stage + 2]
        spot = lane if origin is None else origin
        high_a = (spot >> lane_a) & 1 == 1
        high_b = (spot >> lane_b) & 1 == 1
        shifts = {}

        def moved_by(value, step_a, step_b):
            shift = step_a * (1 << lane_a) + step_b * (1 << lane_b)
            if origin is None:
                return value if shift == 0 else pltpu.roll(value, -shift % LANES, 1)
            if shift not in shifts:
                shifts[shift] = (origin + shift) & (LANES - 1)
            return picked(value, shifts[shift])

        out = []
        for index in range(CELLS):
            base = index & ~(bit_a | bit_b)
            own_a, own_b = int(index & bit_a != 0), int(index & bit_b != 0)
            parts = [
                [moved_by(values[base | p * bit_a | q * bit_b], own_a - p, own_b - q) for q in range(2)]
                for p in range(2)
            ]
            rows = [jnp.where(high_b, part[1], part[0]) for part in parts]
            out.append(jnp.where(high_a, rows[1], rows[0]))
        values = out
    for index, value in enumerate(values):
        store(cell_of(index), value)


def lane_of(slot, outer_j, outer_k):
    return (
        (outer_j & 1) << 6
        | (slot >> 2) << 5
        | ((slot >> 1) & 1) << 4
        | outer_k << 2
        | (slot & 1) << 1
        | outer_j >> 1
    )


def lane_routes(table, sub):
    lane = lax.broadcasted_iota(jnp.int32, (8, LANES), 1)
    row = lax.broadcasted_iota(jnp.int32, (8, LANES), 0)
    slot = ((lane >> 5) & 1) << 2 | ((lane >> 4) & 1) << 1 | (lane >> 1) & 1
    outer_j = (lane & 1) << 1 | lane >> 6
    outer_k = (lane >> 2) & 3
    named = []
    for face in range(6):
        column = jnp.broadcast_to(table[:, face : face + 1], (8, LANES))
        picked = jnp.sum(jnp.where(slot == row, column, 0), axis=0, keepdims=True)
        named.append(jnp.broadcast_to(picked, (8, LANES)))

    def inside(edge, face, within, wrapped):
        other = lane_of(named[face] & 7, *wrapped)
        other = jnp.where(named[face] < 0, LANES, other)
        return jnp.where(edge, other, lane_of(slot, *within))

    routes = [
        inside(outer_j == 0, 2, (outer_j - 1, outer_k), (3, outer_k)),
        inside(outer_j == 3, 3, (outer_j + 1, outer_k), (0, outer_k)),
        inside(outer_k == 0, 4, (outer_j, outer_k - 1), (outer_j, 3)),
        inside(outer_k == 3, 5, (outer_j, outer_k + 1), (outer_j, 0)),
    ]
    low = lane_of(named[0] & 7, outer_j, outer_k)
    high = lane_of(named[1] & 7, outer_j, outer_k)
    routes.append(jnp.where(sub == 0, high, low))
    routes.append(jnp.where(sub == 0, low, high))
    return routes


def picked(value, lanes):
    return jnp.take_along_axis(value, lanes, axis=1, mode="promise_in_bounds")


def halves_kernel(field, far_half, chip_half, far_done, chip_done):
    sub = lax.axis_index("sub")
    moves = []
    for target, start, done in (
        (far_half, sub * 8, far_done),
        (chip_half, 8 - sub * 8, chip_done),
    ):
        rows = pl.ds(pl.multiple_of(start, 8), 8)
        move = pltpu.make_async_copy(field.at[:, rows, :], target, done)
        move.start()
        moves.append(move)
    for move in moves:
        move.wait()


def merge_kernel(near, far, field):
    sub = lax.axis_index("sub")
    for planes, start in ((near, 8 - sub * 8), (far, sub * 8)):
        rows = pl.ds(pl.multiple_of(start, 8), 8)
        values = swap_bits([planes[cell_of(index)] for index in range(CELLS)])
        for index, value in enumerate(values):
            columns = slice((index >> 3) * LANES, (index >> 3) * LANES + LANES)
            field[0, index & 7, rows, columns] = value


def face_routes(routes):
    return [(route < LANES, route & (LANES - 1)) for route in routes[:4]]


def around(center, side_a, side_b, faces):
    def across(face, own, other):
        inner, lanes = faces[face]
        return jnp.where(inner, picked(other, lanes), own)

    cells = [center(cell) for cell in range(CELLS)]
    for cell in range(CELLS):
        value = cells[cell]
        inner_j, inner_k = cell // 4, cell % 4
        total = side_a(cell) + side_b(cell)
        below = cells[cell - 4] if inner_j > 0 else across(0, value, cells[cell + 12])
        above = cells[cell + 4] if inner_j < 3 else across(1, value, cells[cell - 12])
        before = cells[cell - 1] if inner_k > 0 else across(2, value, cells[cell + 3])
        behind = cells[cell + 1] if inner_k < 3 else across(3, value, cells[cell - 3])
        yield cell, value, (total + (below + above)) + (before + behind)


def around_at(source, start, step, faces):
    return around(
        lambda cell: source[cell, pl.ds(start, 8)],
        lambda cell: source[cell, pl.ds(start - step, 8)],
        lambda cell: source[cell, pl.ds(start + step, 8)],
        faces,
    )


class Scheme:
    def __init__(self, nodes, weights, points):
        one, six = np.float32(1.0), np.float32(6.0)
        self.nodes = nodes
        self.weights = weights
        self.stiffness = [np.float32(diffusion) * points[n] for n in range(nodes)]
        self.scales = [one / (one + six * a) for a in self.stiffness]
        self.whole = [np.float32(np.sum(weights[n].astype(np.float64))) for n in range(nodes)]
        self.count = 5 * nodes + 5

    def field(self, level, node=0):
        if level == 0:
            return 0
        if level <= JACOBI:
            return 1 + (level - 1) * self.nodes + node
        return JACOBI * self.nodes + level - JACOBI

    def right(self, sweep, node=0):
        return JACOBI * self.nodes + JACOBI + (node if sweep == 0 else self.nodes)

    def own(self, node, values):
        chosen = jnp.float32(values[0])
        for n in range(1, self.nodes):
            chosen = jnp.where(node == n, jnp.float32(values[n]), chosen)
        return chosen

    def first_step(self, value, total):
        laplace = total - 6.0 * value
        force = diffusion * laplace + reaction * value * (1.0 - value * value)
        for n in range(self.nodes):
            right = (value + self.whole[n] * force - self.stiffness[n] * laplace) * self.scales[n]
            yield n, right, value + (self.whole[n] * self.scales[n]) * force

    def second_step(self, node, start, steps):
        stiffness = self.own(node, self.stiffness)
        scale = self.own(node, self.scales)
        integral = start
        own_value, own_laplace = None, None
        for n, (_, value, total) in enumerate(steps):
            laplace = total - 6.0 * value
            force = diffusion * laplace + reaction * value * (1.0 - value * value)
            weight = self.own(node, [self.weights[m, n] for m in range(self.nodes)])
            integral = integral + weight * force
            own_value = value if n == 0 else jnp.where(node == n, value, own_value)
            own_laplace = laplace if n == 0 else jnp.where(node == n, laplace, own_laplace)
        right = (integral - stiffness * own_laplace) * scale
        return right, (integral + (6.0 * stiffness) * own_value) * scale

    def factor(self, node, sweep, n):
        if sweep == 0:
            return self.stiffness[n] * self.scales[n]
        return self.own(node, self.stiffness) * self.own(node, self.scales)


def near_kernel(scheme, chip_half, far_half, chip_got, table, edges, mirror, planes, sums, lanes, state):
    sub = lax.axis_index("sub")
    node = lax.axis_index("node")
    nodes = scheme.nodes
    routes = lane_routes(table, sub)
    for index, route in enumerate(routes):
        lanes[index] = route
    faces = face_routes(routes)
    below, above = slice(0, 8), slice(16, 24)
    low_half = pl.ds(pl.multiple_of(sub * 16, 8), 8)
    chip_half_rows = pl.ds(8, 8)
    high_half = pl.ds(pl.multiple_of(16 - sub * 16, 8), 8)

    def store_far(cell, value):
        state[0, cell, low_half] = value
        edges[0, cell, above] = value
        edges[0, cell, below] = value

    def store_chip(cell, value):
        state[0, cell, chip_half_rows] = value

    def store_got(cell, value):
        state[0, cell, high_half] = value

    spread(far_half, store_far)
    spread(chip_half, store_chip)
    spread_to(chip_got, routes[4], store_got)
    for row in range(8):
        mirror[:, 7 - row : 8 - row, :] = edges[0, :, row : row + 1, :]

    span = EDGE + 8

    def starts(level):
        count = -(-(span - 2 * level) // 8)
        if count == 1:
            return [level]
        return [level + round(piece * (span - 2 * level - 8) / (count - 1)) for piece in range(count)]

    def keep(index, level, start, cell, value):
        state[index, cell, pl.ds(start, 8)] = value
        if start == level:
            edges[index, cell, above] = value
        if start == span - 8 - level:
            edges[index, cell, below] = value

    for start in starts(1):
        for cell, value, total in around_at(state.at[0], start, 1, faces):
            for n, right, update in scheme.first_step(value, total):
                keep(scheme.right(0, n), 1, start, cell, right)
                keep(scheme.field(1, n), 1, start, cell, update)
    for level in range(2, JACOBI + 1):
        for start in starts(level):
            for n in range(nodes):
                factor = scheme.factor(node, 0, n)
                for cell, value, total in around_at(state.at[scheme.field(level - 1, n)], start, 1, faces):
                    right = state[scheme.right(0, n), cell, pl.ds(start, 8)]
                    keep(scheme.field(level, n), level, start, cell, right + factor * total)
    level = JACOBI + 1
    for start in starts(level):
        sources = [state.at[scheme.field(JACOBI, n)] for n in range(nodes)]
        for steps in zip(*[around_at(source, start, 1, faces) for source in sources]):
            cell = steps[0][0]
            right, update = scheme.second_step(node, state[0, cell, pl.ds(start, 8)], steps)
            keep(scheme.right(1), level, start, cell, right)
            keep(scheme.field(level), level, start, cell, update)
    factor = scheme.factor(node, 1, 0)
    for level in range(JACOBI + 2, 2 * JACOBI):
        for start in starts(level):
            for cell, value, total in around_at(state.at[scheme.field(level - 1)], start, 1, faces):
                right = state[scheme.right(1), cell, pl.ds(start, 8)]
                keep(scheme.field(level), level, start, cell, right + factor * total)
    first_squares, second_squares = [], []
    start = 2 * JACOBI
    rows = pl.ds(start, 8)
    earlier_place = scheme.field(JACOBI) + node
    for cell, value, total in around_at(state.at[scheme.field(start - 1)], start, 1, faces):
        update = state[scheme.right(1), cell, rows] + factor * total
        planes[cell] = update
        earlier = state[earlier_place, cell, rows]
        change = update - earlier
        second_squares.append(change * change)
        change = earlier - state[0, cell, rows]
        first_squares.append(change * change)
    sums[0] = added(first_squares)
    sums[1] = added(second_squares)


def far_kernel(scheme, far_got, edges, mirror, near_sums, lanes, planes, sums, state):
    sub = lax.axis_index("sub")
    for side in range(2):

        @pl.when(sub == side)
        def _():
            far_side(scheme, side, far_got, mirror, near_sums, lanes, planes, sums, state)


def far_side(scheme, side, far_got, mirror, near_sums, lanes, planes, sums, state):
    curve = lax.axis_index("curve")
    node = lax.axis_index("node")
    nodes = scheme.nodes
    faces = face_routes([lanes[index] for index in range(4)])
    toward = 1 - 2 * side
    at_end = curve == (0 if side == 0 else lax.axis_size("curve") - 1)
    new = pl.ds(8, 8)

    def store_far(cell, value):
        state[0, cell, new] = jnp.where(at_end, mirror[cell], value)

    spread_to(far_got, lanes[5], store_far)

    def shifted(levels):
        return pl.ds(8 + toward * levels, 8)

    def ring(index):
        source = state.at[index]
        return around(
            lambda cell: source[cell, shifted(1)],
            lambda cell: source[cell, new],
            lambda cell: source[cell, shifted(2)],
            faces,
        )

    def write(pending):
        for index, cell, value in pending:
            state[index, cell, new] = value

    pending = []
    for cell, value, total in ring(0):
        for n, right, update in scheme.first_step(value, total):
            pending.append((scheme.right(0, n), cell, right))
            pending.append((scheme.field(1, n), cell, update))
    write(pending)
    for level in range(2, JACOBI + 1):
        pending = []
        for n in range(nodes):
            factor = scheme.factor(node, 0, n)
            for cell, value, total in ring(scheme.field(level - 1, n)):
                right = state[scheme.right(0, n), cell, shifted(level - 1)]
                pending.append((scheme.field(level, n), cell, right + factor * total))
        write(pending)
    level = JACOBI + 1
    pending = []
    for steps in zip(*[ring(scheme.field(JACOBI, n)) for n in range(nodes)]):
        cell = steps[0][0]
        right, update = scheme.second_step(node, state[0, cell, shifted(level)], steps)
        pending.append((scheme.right(1), cell, right))
        pending.append((scheme.field(level), cell, update))
    write(pending)
    factor = scheme.factor(node, 1, 0)
    for level in range(JACOBI + 2, 2 * JACOBI):
        pending = []
        for cell, value, total in ring(scheme.field(level - 1)):
            right = state[scheme.right(1), cell, shifted(level - JACOBI - 1)]
            pending.append((scheme.field(level), cell, right + factor * total))
        write(pending)
    level = 2 * JACOBI
    first_squares, second_squares = [near_sums[0]], [near_sums[1]]
    for cell, value, total in ring(scheme.field(level - 1)):
        update = state[scheme.right(1), cell, shifted(JACOBI - 1)] + factor * total
        planes[cell] = update
        earlier = state[scheme.field(JACOBI) + node, cell, shifted(JACOBI)]
        change = update - earlier
        second_squares.append(change * change)
        change = earlier - state[0, cell, shifted(level)]
        first_squares.append(change * change)
    sums[0:1, :] = jnp.sum(added(first_squares), axis=0, keepdims=True)
    sums[1:2, :] = jnp.sum(added(second_squares), axis=0, keepdims=True)


def norm_kernel(cells, sums, got, norms):
    totals = jnp.sum(sums[...] + got[...], axis=1, keepdims=True)
    lane = lax.broadcasted_iota(jnp.int32, (1, 2), 1)
    norms[...] = jnp.sqrt(jnp.where(lane == 0, totals[0:1], totals[1:2]) / cells + 1e-06)


def added(terms):
    while len(terms) > 1:
        terms = [sum(terms[place + 1 : place + 2], terms[place]) for place in range(0, len(terms), 2)]
    return terms[0]


def pairs_over(sizes, partner):
    pairs = []
    for index in np.ndindex(*sizes):
        other = partner(*[int(i) for i in index])
        if other is not None:
            pairs.append((int(np.ravel_multi_index(index, sizes)), int(np.ravel_multi_index(other, sizes))))
    return pairs


def shards(start_field, neighbours):
    nodes = lax.axis_size("node")
    axes = ("curve", "node", "sub")
    sizes = tuple(lax.axis_size(axis) for axis in axes)
    chips = sizes[0]
    scheme = Scheme(nodes, *radau_tables(nodes))
    half = jax.ShapeDtypeStruct((8, 8, EDGE * EDGE), jnp.float32)
    planes = jax.ShapeDtypeStruct((CELLS, 8, LANES), jnp.float32)
    limit = pltpu.CompilerParams(vmem_limit_bytes=24 * 1024 * 1024)

    def across(curve, node, sub):
        if sub == 1 and curve + 1 < chips:
            return (curve + 1, node, 0)
        if sub == 0 and curve > 0:
            return (curve - 1, node, 1)
        return (curve, node ^ 1, sub) if node ^ 1 < nodes else None

    def beside(bit, swap):
        def partner(curve, node, sub):
            return (curve ^ bit, node, sub ^ swap)

        return partner

    def moved(value, partner):
        return lax.ppermute(value, axes, pairs_over(sizes, partner))

    far_half, chip_half = pl.pallas_call(
        halves_kernel,
        out_shape=[half, half],
        in_specs=[pl.BlockSpec(memory_space=pltpu.HBM)],
        out_specs=[VMEM, VMEM],
        scratch_shapes=[pltpu.SemaphoreType.DMA, pltpu.SemaphoreType.DMA],
        compiler_params=limit,
    )(start_field)
    far_got = moved(far_half, across)
    chip_got = moved(chip_half, beside(0, 1))
    shared = jax.ShapeDtypeStruct((scheme.count, CELLS, EDGE + 8, LANES), jnp.float32)
    edges, mirror, near_planes, near_sums, lanes = pl.pallas_call(
        functools.partial(near_kernel, scheme),
        out_shape=[
            shared,
            planes,
            planes,
            jax.ShapeDtypeStruct((2, 8, LANES), jnp.float32),
            jax.ShapeDtypeStruct((6, 8, LANES), jnp.int32),
        ],
        in_specs=[VMEM] * 4,
        out_specs=[VMEM] * 5,
        scratch_shapes=[pltpu.VMEM(shared.shape, jnp.float32)],
        compiler_params=limit,
        cost_estimate=pl.CostEstimate(flops=8_000_000, bytes_accessed=2_000_000, transcendentals=0),
    )(chip_half, far_half, chip_got, neighbours)
    far_planes, sums, _ = pl.pallas_call(
        functools.partial(far_kernel, scheme),
        out_shape=[planes, jax.ShapeDtypeStruct((2, LANES), jnp.float32), shared],
        in_specs=[VMEM] * 5,
        out_specs=[VMEM] * 3,
        input_output_aliases={1: 2},
        compiler_params=limit,
    )(far_got, edges, mirror, near_sums, lanes)
    field = pl.pallas_call(
        merge_kernel,
        out_shape=jax.ShapeDtypeStruct((1, 8, EDGE, EDGE * EDGE), jnp.float32),
        in_specs=[VMEM, VMEM],
        out_specs=VMEM,
        compiler_params=limit,
    )(near_planes, far_planes)
    rounds = [beside(0, 1)]
    bit = 1
    while bit < chips:
        rounds.append(beside(bit, 1))
        bit *= 2
    for partner in rounds[:-1]:
        sums = sums + moved(sums, partner)
    cells = start_field.size * chips * sizes[2]
    increments = pl.pallas_call(
        functools.partial(norm_kernel, np.float32(cells)),
        out_shape=jax.ShapeDtypeStruct((1, SWEEPS), jnp.float32),
        in_specs=[VMEM, VMEM],
        out_specs=VMEM,
        compiler_params=limit,
    )(sums, moved(sums, rounds[-1]))
    return (field, increments.T)


def solution(mesh):
    placed = (P(("slab", "curve", "sub"), None, None), P(("slab", "curve", "sub"), None))
    return jax.shard_map(
        shards,
        mesh=mesh,
        in_specs=placed,
        out_specs=(P("node", ("slab", "curve", "sub"), None, None), P("slab", "node")),
        check_vma=False,
    )
```

```python
import functools

import jax
import jax.numpy as jnp
import numpy as np
from jax import lax
from jax.experimental import pallas as pl
from jax.experimental.pallas import tpu as pltpu
from jax.sharding import PartitionSpec as P

SWEEPS = 2
JACOBI = 4

diffusion = 0.5
reaction = 1.0
EDGE = 16
LANES = 128
CELLS = 16
SWAPS = ((4, 5), (2, 4), (1, 1), (8, 0))
VMEM = pl.BlockSpec(memory_space=pltpu.VMEM)


def legendre_value(order, place):
    before = 1.0
    current = place
    for degree in range(1, order):
        following = ((2 * degree + 1) * place * current - degree * before) / (degree + 1)
        before = current
        current = following
    return current


def radau_residue(node_count, moment):
    place = 2.0 * moment - 1.0
    return legendre_value(node_count, place) - legendre_value(node_count - 1, place)


def radau_tables(node_count):
    samples = 4000
    points = []
    for sample in range(samples - 1):
        left_end = sample / samples
        right_end = (sample + 1) / samples
        left_value = radau_residue(node_count, left_end)
        right_value = radau_residue(node_count, right_end)
        if left_value * right_value < 0.0:
            for halving in range(80):
                middle = 0.5 * (left_end + right_end)
                middle_value = radau_residue(node_count, middle)
                if left_value * middle_value <= 0.0:
                    right_end = middle
                else:
                    left_end = middle
                    left_value = middle_value
            points.append(0.5 * (left_end + right_end))
    points.append(1.0)
    table = []
    for row_node in range(node_count):
        table_row = []
        for col_node in range(node_count):
            factors = [1.0]
            for other_node in range(node_count):
                if other_node != col_node:
                    scale = 1.0 / (points[col_node] - points[other_node])
                    shifted = [0.0] + factors
                    product = [
                        shifted[place]
                        - points[other_node] * (factors[place] if place < len(factors) else 0.0)
                        for place in range(len(shifted))
                    ]
                    factors = [entry * scale for entry in product]
            integral = 0.0
            for power_index in range(len(factors)):
                integral = integral + factors[power_index] * points[row_node] ** (
                    power_index + 1
                ) / (power_index + 1)
            table_row.append(integral)
        table.append(table_row)
    return (np.array(table, dtype=np.float32), np.array(points, dtype=np.float32))


def swap_bits(values):
    lane = lax.broadcasted_iota(jnp.int32, (8, LANES), 1)
    for register_bit, lane_bit in SWAPS:
        shift = 1 << lane_bit
        high = (lane >> lane_bit) & 1 == 1
        out = list(values)
        for index in range(CELLS):
            if index & register_bit == 0:
                low_value, high_value = values[index], values[index | register_bit]
                out[index] = jnp.where(high, pltpu.roll(high_value, shift, 1), low_value)
                out[index | register_bit] = jnp.where(
                    high, high_value, pltpu.roll(low_value, LANES - shift, 1)
                )
        values = out
    return values


def cell_of(index):
    return ((index >> 1) & 3) * 4 + ((index & 1) << 1 | index >> 3)


def spread(source, store):
    values = [source[index & 7, :, (index >> 3) * LANES : (index >> 3) * LANES + LANES] for index in range(CELLS)]
    for index, value in enumerate(swap_bits(values)):
        store(cell_of(index), value)


def spread_to(source, route, store):
    lane = lax.broadcasted_iota(jnp.int32, (8, LANES), 1)
    values = [source[index & 7, :, (index >> 3) * LANES : (index >> 3) * LANES + LANES] for index in range(CELLS)]
    for stage, origin in ((0, None), (2, route)):
        (bit_a, lane_a), (bit_b, lane_b) = SWAPS[stage : stage + 2]
        spot = lane if origin is None else origin
        high_a = (spot >> lane_a) & 1 == 1
        high_b = (spot >> lane_b) & 1 == 1
        shifts = {}

        def moved_by(value, step_a, step_b):
            shift = step_a * (1 << lane_a) + step_b * (1 << lane_b)
            if origin is None:
                return value if shift == 0 else pltpu.roll(value, -shift % LANES, 1)
            if shift not in shifts:
                shifts[shift] = (origin + shift) & (LANES - 1)
            return picked(value, shifts[shift])

        out = []
        for index in range(CELLS):
            base = index & ~(bit_a | bit_b)
            own_a, own_b = int(index & bit_a != 0), int(index & bit_b != 0)
            parts = [
                [moved_by(values[base | p * bit_a | q * bit_b], own_a - p, own_b - q) for q in range(2)]
                for p in range(2)
            ]
            rows = [jnp.where(high_b, part[1], part[0]) for part in parts]
            out.append(jnp.where(high_a, rows[1], rows[0]))
        values = out
    for index, value in enumerate(values):
        store(cell_of(index), value)


def lane_of(slot, outer_j, outer_k):
    return (
        (outer_j & 1) << 6
        | (slot >> 2) << 5
        | ((slot >> 1) & 1) << 4
        | outer_k << 2
        | (slot & 1) << 1
        | outer_j >> 1
    )


def lane_routes(table, sub):
    lane = lax.broadcasted_iota(jnp.int32, (8, LANES), 1)
    row = lax.broadcasted_iota(jnp.int32, (8, LANES), 0)
    slot = ((lane >> 5) & 1) << 2 | ((lane >> 4) & 1) << 1 | (lane >> 1) & 1
    outer_j = (lane & 1) << 1 | lane >> 6
    outer_k = (lane >> 2) & 3
    named = []
    for face in range(6):
        column = jnp.broadcast_to(table[:, face : face + 1], (8, LANES))
        picked = jnp.sum(jnp.where(slot == row, column, 0), axis=0, keepdims=True)
        named.append(jnp.broadcast_to(picked, (8, LANES)))

    def inside(edge, face, within, wrapped):
        other = lane_of(named[face] & 7, *wrapped)
        other = jnp.where(named[face] < 0, LANES, other)
        return jnp.where(edge, other, lane_of(slot, *within))

    routes = [
        inside(outer_j == 0, 2, (outer_j - 1, outer_k), (3, outer_k)),
        inside(outer_j == 3, 3, (outer_j + 1, outer_k), (0, outer_k)),
        inside(outer_k == 0, 4, (outer_j, outer_k - 1), (outer_j, 3)),
        inside(outer_k == 3, 5, (outer_j, outer_k + 1), (outer_j, 0)),
    ]
    low = lane_of(named[0] & 7, outer_j, outer_k)
    high = lane_of(named[1] & 7, outer_j, outer_k)
    routes.append(jnp.where(sub == 0, high, low))
    routes.append(jnp.where(sub == 0, low, high))
    return routes


def picked(value, lanes):
    return jnp.take_along_axis(value, lanes, axis=1, mode="promise_in_bounds")


def halves_kernel(field, far_half, chip_half, far_done, chip_done):
    sub = lax.axis_index("sub")
    moves = []
    for target, start, done in (
        (far_half, sub * 8, far_done),
        (chip_half, 8 - sub * 8, chip_done),
    ):
        rows = pl.ds(pl.multiple_of(start, 8), 8)
        move = pltpu.make_async_copy(field.at[:, rows, :], target, done)
        move.start()
        moves.append(move)
    for move in moves:
        move.wait()


def merge_kernel(near, far, field):
    sub = lax.axis_index("sub")
    for planes, start in ((near, 8 - sub * 8), (far, sub * 8)):
        rows = pl.ds(pl.multiple_of(start, 8), 8)
        values = swap_bits([planes[cell_of(index)] for index in range(CELLS)])
        for index, value in enumerate(values):
            columns = slice((index >> 3) * LANES, (index >> 3) * LANES + LANES)
            field[0, index & 7, rows, columns] = value


def face_routes(routes):
    return [(route < LANES, route & (LANES - 1)) for route in routes[:4]]


def around(center, side_a, side_b, faces):
    def across(face, own, other):
        inner, lanes = faces[face]
        return jnp.where(inner, picked(other, lanes), own)

    cells = [center(cell) for cell in range(CELLS)]
    rim = [cell for cell in range(CELLS) if cell // 4 in (0, 3) or cell % 4 in (0, 3)]
    for cell in rim + [5, 6, 9, 10]:
        value = cells[cell]
        inner_j, inner_k = cell // 4, cell % 4
        total = side_a(cell) + side_b(cell)
        below = cells[cell - 4] if inner_j > 0 else across(0, value, cells[cell + 12])
        above = cells[cell + 4] if inner_j < 3 else across(1, value, cells[cell - 12])
        before = cells[cell - 1] if inner_k > 0 else across(2, value, cells[cell + 3])
        behind = cells[cell + 1] if inner_k < 3 else across(3, value, cells[cell - 3])
        yield cell, value, (total + (below + above)) + (before + behind)


def around_at(source, start, step, faces):
    return around(
        lambda cell: source[cell, pl.ds(start, 8)],
        lambda cell: source[cell, pl.ds(start - step, 8)],
        lambda cell: source[cell, pl.ds(start + step, 8)],
        faces,
    )


class Scheme:
    def __init__(self, nodes, weights, points):
        one, six = np.float32(1.0), np.float32(6.0)
        self.nodes = nodes
        self.weights = weights
        self.stiffness = [np.float32(diffusion) * points[n] for n in range(nodes)]
        self.scales = [one / (one + six * a) for a in self.stiffness]
        self.whole = [np.float32(np.sum(weights[n].astype(np.float64))) for n in range(nodes)]
        self.count = 5 * nodes + 5

    def field(self, level, node=0):
        if level == 0:
            return 0
        if level <= JACOBI:
            return 1 + (level - 1) * self.nodes + node
        return JACOBI * self.nodes + level - JACOBI

    def right(self, sweep, node=0):
        return JACOBI * self.nodes + JACOBI + (node if sweep == 0 else self.nodes)

    def own(self, node, values):
        chosen = jnp.float32(values[0])
        for n in range(1, self.nodes):
            chosen = jnp.where(node == n, jnp.float32(values[n]), chosen)
        return chosen

    def first_step(self, value, total):
        laplace = total - 6.0 * value
        force = diffusion * laplace + reaction * value * (1.0 - value * value)
        for n in range(self.nodes):
            right = (value + self.whole[n] * force - self.stiffness[n] * laplace) * self.scales[n]
            yield n, right, value + (self.whole[n] * self.scales[n]) * force

    def second_step(self, node, start, steps):
        stiffness = self.own(node, self.stiffness)
        scale = self.own(node, self.scales)
        integral = start
        own_value, own_laplace = None, None
        for n, (_, value, total) in enumerate(steps):
            laplace = total - 6.0 * value
            force = diffusion * laplace + reaction * value * (1.0 - value * value)
            weight = self.own(node, [self.weights[m, n] for m in range(self.nodes)])
            integral = integral + weight * force
            own_value = value if n == 0 else jnp.where(node == n, value, own_value)
            own_laplace = laplace if n == 0 else jnp.where(node == n, laplace, own_laplace)
        right = (integral - stiffness * own_laplace) * scale
        return right, (integral + (6.0 * stiffness) * own_value) * scale

    def factor(self, node, sweep, n):
        if sweep == 0:
            return self.stiffness[n] * self.scales[n]
        return self.own(node, self.stiffness) * self.own(node, self.scales)


def near_kernel(scheme, chip_half, far_half, chip_got, table, edges, mirror, planes, sums, lanes, state):
    sub = lax.axis_index("sub")
    node = lax.axis_index("node")
    nodes = scheme.nodes
    routes = lane_routes(table, sub)
    for index, route in enumerate(routes):
        lanes[index] = route
    faces = face_routes(routes)
    below, above = slice(0, 8), slice(16, 24)
    low_half = pl.ds(pl.multiple_of(sub * 16, 8), 8)
    chip_half_rows = pl.ds(8, 8)
    high_half = pl.ds(pl.multiple_of(16 - sub * 16, 8), 8)

    def store_far(cell, value):
        state[0, cell, low_half] = value
        edges[0, cell, above] = value
        edges[0, cell, below] = value

    def store_chip(cell, value):
        state[0, cell, chip_half_rows] = value

    def store_got(cell, value):
        state[0, cell, high_half] = value

    spread(far_half, store_far)
    spread(chip_half, store_chip)
    spread_to(chip_got, routes[4], store_got)
    for row in range(8):
        mirror[:, 7 - row : 8 - row, :] = edges[0, :, row : row + 1, :]

    span = EDGE + 8

    def starts(level):
        count = -(-(span - 2 * level) // 8)
        if count == 1:
            return [level]
        return [level + round(piece * (span - 2 * level - 8) / (count - 1)) for piece in range(count)]

    def keep(index, level, start, cell, value):
        state[index, cell, pl.ds(start, 8)] = value
        if start == level:
            edges[index, cell, above] = value
        if start == span - 8 - level:
            edges[index, cell, below] = value

    for start in starts(1):
        for cell, value, total in around_at(state.at[0], start, 1, faces):
            for n, right, update in scheme.first_step(value, total):
                keep(scheme.right(0, n), 1, start, cell, right)
                keep(scheme.field(1, n), 1, start, cell, update)
    for level in range(2, JACOBI + 1):
        for start in starts(level):
            for n in range(nodes):
                factor = scheme.factor(node, 0, n)
                for cell, value, total in around_at(state.at[scheme.field(level - 1, n)], start, 1, faces):
                    right = state[scheme.right(0, n), cell, pl.ds(start, 8)]
                    keep(scheme.field(level, n), level, start, cell, right + factor * total)
    level = JACOBI + 1
    for start in starts(level):
        sources = [state.at[scheme.field(JACOBI, n)] for n in range(nodes)]
        for steps in zip(*[around_at(source, start, 1, faces) for source in sources]):
            cell = steps[0][0]
            right, update = scheme.second_step(node, state[0, cell, pl.ds(start, 8)], steps)
            keep(scheme.right(1), level, start, cell, right)
            keep(scheme.field(level), level, start, cell, update)
    factor = scheme.factor(node, 1, 0)
    for level in range(JACOBI + 2, 2 * JACOBI):
        for start in starts(level):
            for cell, value, total in around_at(state.at[scheme.field(level - 1)], start, 1, faces):
                right = state[scheme.right(1), cell, pl.ds(start, 8)]
                keep(scheme.field(level), level, start, cell, right + factor * total)
    first_squares, second_squares = [], []
    start = 2 * JACOBI
    rows = pl.ds(start, 8)
    earlier_place = scheme.field(JACOBI) + node
    for cell, value, total in around_at(state.at[scheme.field(start - 1)], start, 1, faces):
        update = state[scheme.right(1), cell, rows] + factor * total
        planes[cell] = update
        earlier = state[earlier_place, cell, rows]
        change = update - earlier
        second_squares.append(change * change)
        change = earlier - state[0, cell, rows]
        first_squares.append(change * change)
    sums[0] = added(first_squares)
    sums[1] = added(second_squares)


def far_kernel(scheme, far_got, edges, mirror, near_sums, lanes, planes, sums, state):
    sub = lax.axis_index("sub")
    for side in range(2):

        @pl.when(sub == side)
        def _():
            far_side(scheme, side, far_got, mirror, near_sums, lanes, planes, sums, state)


def far_side(scheme, side, far_got, mirror, near_sums, lanes, planes, sums, state):
    curve = lax.axis_index("curve")
    node = lax.axis_index("node")
    nodes = scheme.nodes
    faces = face_routes([lanes[index] for index in range(4)])
    toward = 1 - 2 * side
    at_end = curve == (0 if side == 0 else lax.axis_size("curve") - 1)
    new = pl.ds(8, 8)

    def store_far(cell, value):
        state[0, cell, new] = jnp.where(at_end, mirror[cell], value)

    spread_to(far_got, lanes[5], store_far)

    def shifted(levels):
        return pl.ds(8 + toward * levels, 8)

    def ring(index):
        source = state.at[index]
        return around(
            lambda cell: source[cell, shifted(1)],
            lambda cell: source[cell, new],
            lambda cell: source[cell, shifted(2)],
            faces,
        )

    def write(pending):
        for index, cell, value in pending:
            state[index, cell, new] = value

    pending = []
    for cell, value, total in ring(0):
        for n, right, update in scheme.first_step(value, total):
            pending.append((scheme.right(0, n), cell, right))
            pending.append((scheme.field(1, n), cell, update))
    write(pending)
    for level in range(2, JACOBI + 1):
        pending = []
        for n in range(nodes):
            factor = scheme.factor(node, 0, n)
            for cell, value, total in ring(scheme.field(level - 1, n)):
                right = state[scheme.right(0, n), cell, shifted(level - 1)]
                pending.append((scheme.field(level, n), cell, right + factor * total))
        write(pending)
    level = JACOBI + 1
    pending = []
    for steps in zip(*[ring(scheme.field(JACOBI, n)) for n in range(nodes)]):
        cell = steps[0][0]
        right, update = scheme.second_step(node, state[0, cell, shifted(level)], steps)
        pending.append((scheme.right(1), cell, right))
        pending.append((scheme.field(level), cell, update))
    write(pending)
    factor = scheme.factor(node, 1, 0)
    for level in range(JACOBI + 2, 2 * JACOBI):
        pending = []
        for cell, value, total in ring(scheme.field(level - 1)):
            right = state[scheme.right(1), cell, shifted(level - JACOBI - 1)]
            pending.append((scheme.field(level), cell, right + factor * total))
        write(pending)
    level = 2 * JACOBI
    first_squares, second_squares = [near_sums[0]], [near_sums[1]]
    for cell, value, total in ring(scheme.field(level - 1)):
        update = state[scheme.right(1), cell, shifted(JACOBI - 1)] + factor * total
        planes[cell] = update
        earlier = state[scheme.field(JACOBI) + node, cell, shifted(JACOBI)]
        change = update - earlier
        second_squares.append(change * change)
        change = earlier - state[0, cell, shifted(level)]
        first_squares.append(change * change)
    first, second = added(first_squares), added(second_squares)
    row = lax.broadcasted_iota(jnp.int32, (8, LANES), 0)
    both = jnp.where(row < 4, first + pltpu.roll(first, 4, 0), second + pltpu.roll(second, 4, 0))
    both = both + pltpu.roll(both, 6, 0)
    both = both + pltpu.roll(both, 7, 0)
    sums[0:1, :] = both[0:1]
    sums[1:2, :] = both[4:5]


def norm_kernel(cells, sums, got, norms):
    totals = jnp.sum(sums[...] + got[...], axis=1, keepdims=True)
    lane = lax.broadcasted_iota(jnp.int32, (1, 2), 1)
    norms[...] = jnp.sqrt(jnp.where(lane == 0, totals[0:1], totals[1:2]) / cells + 1e-06)


def added(terms):
    while len(terms) > 1:
        terms = [sum(terms[place + 1 : place + 2], terms[place]) for place in range(0, len(terms), 2)]
    return terms[0]


def pairs_over(sizes, partner):
    pairs = []
    for index in np.ndindex(*sizes):
        other = partner(*[int(i) for i in index])
        if other is not None:
            pairs.append((int(np.ravel_multi_index(index, sizes)), int(np.ravel_multi_index(other, sizes))))
    return pairs


def shards(start_field, neighbours):
    nodes = lax.axis_size("node")
    axes = ("curve", "node", "sub")
    sizes = tuple(lax.axis_size(axis) for axis in axes)
    chips = sizes[0]
    scheme = Scheme(nodes, *radau_tables(nodes))
    half = jax.ShapeDtypeStruct((8, 8, EDGE * EDGE), jnp.float32)
    planes = jax.ShapeDtypeStruct((CELLS, 8, LANES), jnp.float32)
    limit = pltpu.CompilerParams(vmem_limit_bytes=24 * 1024 * 1024)

    def across(curve, node, sub):
        if sub == 1 and curve + 1 < chips:
            return (curve + 1, node, 0)
        if sub == 0 and curve > 0:
            return (curve - 1, node, 1)
        return (curve, node ^ 1, sub) if node ^ 1 < nodes else None

    def beside(bit, swap):
        def partner(curve, node, sub):
            return (curve ^ bit, node, sub ^ swap)

        return partner

    def moved(value, partner):
        return lax.ppermute(value, axes, pairs_over(sizes, partner))

    far_half, chip_half = pl.pallas_call(
        halves_kernel,
        out_shape=[half, half],
        in_specs=[pl.BlockSpec(memory_space=pltpu.HBM)],
        out_specs=[VMEM, VMEM],
        scratch_shapes=[pltpu.SemaphoreType.DMA, pltpu.SemaphoreType.DMA],
        compiler_params=limit,
    )(start_field)
    far_got = moved(far_half, across)
    chip_got = moved(chip_half, beside(0, 1))
    shared = jax.ShapeDtypeStruct((scheme.count, CELLS, EDGE + 8, LANES), jnp.float32)
    edges, mirror, near_planes, near_sums, lanes = pl.pallas_call(
        functools.partial(near_kernel, scheme),
        out_shape=[
            shared,
            planes,
            planes,
            jax.ShapeDtypeStruct((2, 8, LANES), jnp.float32),
            jax.ShapeDtypeStruct((6, 8, LANES), jnp.int32),
        ],
        in_specs=[VMEM] * 4,
        out_specs=[VMEM] * 5,
        scratch_shapes=[pltpu.VMEM(shared.shape, jnp.float32)],
        compiler_params=limit,
        cost_estimate=pl.CostEstimate(flops=8_000_000, bytes_accessed=2_000_000, transcendentals=0),
    )(chip_half, far_half, chip_got, neighbours)
    far_planes, sums, _ = pl.pallas_call(
        functools.partial(far_kernel, scheme),
        out_shape=[planes, jax.ShapeDtypeStruct((2, LANES), jnp.float32), shared],
        in_specs=[VMEM] * 5,
        out_specs=[VMEM] * 3,
        input_output_aliases={1: 2},
        compiler_params=limit,
    )(far_got, edges, mirror, near_sums, lanes)
    field = pl.pallas_call(
        merge_kernel,
        out_shape=jax.ShapeDtypeStruct((1, 8, EDGE, EDGE * EDGE), jnp.float32),
        in_specs=[VMEM, VMEM],
        out_specs=VMEM,
        compiler_params=limit,
    )(near_planes, far_planes)
    rounds = [beside(0, 1)]
    bit = 1
    while bit < chips:
        rounds.append(beside(bit, 1))
        bit *= 2
    for partner in rounds[:-1]:
        sums = sums + moved(sums, partner)
    cells = start_field.size * chips * sizes[2]
    increments = pl.pallas_call(
        functools.partial(norm_kernel, np.float32(cells)),
        out_shape=jax.ShapeDtypeStruct((1, SWEEPS), jnp.float32),
        in_specs=[VMEM, VMEM],
        out_specs=VMEM,
        compiler_params=limit,
    )(sums, moved(sums, rounds[-1]))
    return (field, increments.T)


def solution(mesh):
    placed = (P(("slab", "curve", "sub"), None, None), P(("slab", "curve", "sub"), None))
    return jax.shard_map(
        shards,
        mesh=mesh,
        in_specs=placed,
        out_specs=(P("node", ("slab", "curve", "sub"), None, None), P("slab", "node")),
        check_vma=False,
    )
```

```python
import functools

import jax
import jax.numpy as jnp
import numpy as np
from jax import lax
from jax.experimental import pallas as pl
from jax.experimental.pallas import tpu as pltpu
from jax.sharding import PartitionSpec as P

SWEEPS = 2
JACOBI = 4

diffusion = 0.5
reaction = 1.0
EDGE = 16
LANES = 128
CELLS = 16
SWAPS = ((4, 5), (2, 4), (1, 1), (8, 0))
VMEM = pl.BlockSpec(memory_space=pltpu.VMEM)


def legendre_value(order, place):
    before = 1.0
    current = place
    for degree in range(1, order):
        following = ((2 * degree + 1) * place * current - degree * before) / (degree + 1)
        before = current
        current = following
    return current


def radau_residue(node_count, moment):
    place = 2.0 * moment - 1.0
    return legendre_value(node_count, place) - legendre_value(node_count - 1, place)


def radau_tables(node_count):
    samples = 4000
    points = []
    for sample in range(samples - 1):
        left_end = sample / samples
        right_end = (sample + 1) / samples
        left_value = radau_residue(node_count, left_end)
        right_value = radau_residue(node_count, right_end)
        if left_value * right_value < 0.0:
            for halving in range(80):
                middle = 0.5 * (left_end + right_end)
                middle_value = radau_residue(node_count, middle)
                if left_value * middle_value <= 0.0:
                    right_end = middle
                else:
                    left_end = middle
                    left_value = middle_value
            points.append(0.5 * (left_end + right_end))
    points.append(1.0)
    table = []
    for row_node in range(node_count):
        table_row = []
        for col_node in range(node_count):
            factors = [1.0]
            for other_node in range(node_count):
                if other_node != col_node:
                    scale = 1.0 / (points[col_node] - points[other_node])
                    shifted = [0.0] + factors
                    product = [
                        shifted[place]
                        - points[other_node] * (factors[place] if place < len(factors) else 0.0)
                        for place in range(len(shifted))
                    ]
                    factors = [entry * scale for entry in product]
            integral = 0.0
            for power_index in range(len(factors)):
                integral = integral + factors[power_index] * points[row_node] ** (
                    power_index + 1
                ) / (power_index + 1)
            table_row.append(integral)
        table.append(table_row)
    return (np.array(table, dtype=np.float32), np.array(points, dtype=np.float32))


def swap_bits(values):
    lane = lax.broadcasted_iota(jnp.int32, (8, LANES), 1)
    for register_bit, lane_bit in SWAPS:
        shift = 1 << lane_bit
        high = (lane >> lane_bit) & 1 == 1
        out = list(values)
        for index in range(CELLS):
            if index & register_bit == 0:
                low_value, high_value = values[index], values[index | register_bit]
                out[index] = jnp.where(high, pltpu.roll(high_value, shift, 1), low_value)
                out[index | register_bit] = jnp.where(
                    high, high_value, pltpu.roll(low_value, LANES - shift, 1)
                )
        values = out
    return values


def cell_of(index):
    return ((index >> 1) & 3) * 4 + ((index & 1) << 1 | index >> 3)


def spread(source, store):
    values = [source[index & 7, :, (index >> 3) * LANES : (index >> 3) * LANES + LANES] for index in range(CELLS)]
    for index, value in enumerate(swap_bits(values)):
        store(cell_of(index), value)


def spread_to(source, route, store):
    lane = lax.broadcasted_iota(jnp.int32, (8, LANES), 1)
    values = [source[index & 7, :, (index >> 3) * LANES : (index >> 3) * LANES + LANES] for index in range(CELLS)]
    for stage, origin in ((0, None), (2, route)):
        (bit_a, lane_a), (bit_b, lane_b) = SWAPS[stage : stage + 2]
        spot = lane if origin is None else origin
        high_a = (spot >> lane_a) & 1 == 1
        high_b = (spot >> lane_b) & 1 == 1
        shifts = {}

        def moved_by(value, step_a, step_b):
            shift = step_a * (1 << lane_a) + step_b * (1 << lane_b)
            if origin is None:
                return value if shift == 0 else pltpu.roll(value, -shift % LANES, 1)
            if shift not in shifts:
                shifts[shift] = (origin + shift) & (LANES - 1)
            return picked(value, shifts[shift])

        out = []
        for index in range(CELLS):
            base = index & ~(bit_a | bit_b)
            own_a, own_b = int(index & bit_a != 0), int(index & bit_b != 0)
            parts = [
                [moved_by(values[base | p * bit_a | q * bit_b], own_a - p, own_b - q) for q in range(2)]
                for p in range(2)
            ]
            rows = [jnp.where(high_b, part[1], part[0]) for part in parts]
            out.append(jnp.where(high_a, rows[1], rows[0]))
        values = out
    for index, value in enumerate(values):
        store(cell_of(index), value)


def lane_of(slot, outer_j, outer_k):
    return (
        (outer_j & 1) << 6
        | (slot >> 2) << 5
        | ((slot >> 1) & 1) << 4
        | outer_k << 2
        | (slot & 1) << 1
        | outer_j >> 1
    )


def lane_routes(table, sub):
    lane = lax.broadcasted_iota(jnp.int32, (8, LANES), 1)
    row = lax.broadcasted_iota(jnp.int32, (8, LANES), 0)
    slot = ((lane >> 5) & 1) << 2 | ((lane >> 4) & 1) << 1 | (lane >> 1) & 1
    outer_j = (lane & 1) << 1 | lane >> 6
    outer_k = (lane >> 2) & 3
    named = []
    for face in range(6):
        column = jnp.broadcast_to(table[:, face : face + 1], (8, LANES))
        picked = jnp.sum(jnp.where(slot == row, column, 0), axis=0, keepdims=True)
        named.append(jnp.broadcast_to(picked, (8, LANES)))

    def inside(edge, face, within, wrapped):
        other = lane_of(named[face] & 7, *wrapped)
        other = jnp.where(named[face] < 0, LANES, other)
        return jnp.where(edge, other, lane_of(slot, *within))

    routes = [
        inside(outer_j == 0, 2, (outer_j - 1, outer_k), (3, outer_k)),
        inside(outer_j == 3, 3, (outer_j + 1, outer_k), (0, outer_k)),
        inside(outer_k == 0, 4, (outer_j, outer_k - 1), (outer_j, 3)),
        inside(outer_k == 3, 5, (outer_j, outer_k + 1), (outer_j, 0)),
    ]
    low = lane_of(named[0] & 7, outer_j, outer_k)
    high = lane_of(named[1] & 7, outer_j, outer_k)
    routes.append(jnp.where(sub == 0, high, low))
    routes.append(jnp.where(sub == 0, low, high))
    return routes


def picked(value, lanes):
    return jnp.take_along_axis(value, lanes, axis=1, mode="promise_in_bounds")


def halves_kernel(field, far_half, chip_half, far_done, chip_done):
    sub = lax.axis_index("sub")
    moves = []
    for target, start, done in (
        (far_half, sub * 8, far_done),
        (chip_half, 8 - sub * 8, chip_done),
    ):
        rows = pl.ds(pl.multiple_of(start, 8), 8)
        move = pltpu.make_async_copy(field.at[:, rows, :], target, done)
        move.start()
        moves.append(move)
    for move in moves:
        move.wait()


def merge_kernel(near, far, field):
    sub = lax.axis_index("sub")
    for planes, start in ((near, 8 - sub * 8), (far, sub * 8)):
        rows = pl.ds(pl.multiple_of(start, 8), 8)
        values = swap_bits([planes[cell_of(index)] for index in range(CELLS)])
        for index, value in enumerate(values):
            columns = slice((index >> 3) * LANES, (index >> 3) * LANES + LANES)
            field[0, index & 7, rows, columns] = value


def face_routes(routes):
    return [(route < LANES, route & (LANES - 1)) for route in routes[:4]]


def around(center, side_a, side_b, faces):
    def across(face, own, other):
        inner, lanes = faces[face]
        return jnp.where(inner, picked(other, lanes), own)

    cells = [center(cell) for cell in range(CELLS)]
    for cell in range(CELLS):
        value = cells[cell]
        inner_j, inner_k = cell // 4, cell % 4
        total = side_a(cell) + side_b(cell)
        below = cells[cell - 4] if inner_j > 0 else across(0, value, cells[cell + 12])
        above = cells[cell + 4] if inner_j < 3 else across(1, value, cells[cell - 12])
        before = cells[cell - 1] if inner_k > 0 else across(2, value, cells[cell + 3])
        behind = cells[cell + 1] if inner_k < 3 else across(3, value, cells[cell - 3])
        yield cell, value, (total + (below + above)) + (before + behind)


def around_at(source, start, step, faces):
    return around(
        lambda cell: source[cell, pl.ds(start, 8)],
        lambda cell: source[cell, pl.ds(start - step, 8)],
        lambda cell: source[cell, pl.ds(start + step, 8)],
        faces,
    )


class Scheme:
    def __init__(self, nodes, weights, points):
        one, six = np.float32(1.0), np.float32(6.0)
        self.nodes = nodes
        self.weights = weights
        self.stiffness = [np.float32(diffusion) * points[n] for n in range(nodes)]
        self.scales = [one / (one + six * a) for a in self.stiffness]
        self.whole = [np.float32(np.sum(weights[n].astype(np.float64))) for n in range(nodes)]
        self.count = 5 * nodes + 5

    def field(self, level, node=0):
        if level == 0:
            return 0
        if level <= JACOBI:
            return 1 + (level - 1) * self.nodes + node
        return JACOBI * self.nodes + level - JACOBI

    def right(self, sweep, node=0):
        return JACOBI * self.nodes + JACOBI + (node if sweep == 0 else self.nodes)

    def own(self, node, values):
        chosen = jnp.float32(values[0])
        for n in range(1, self.nodes):
            chosen = jnp.where(node == n, jnp.float32(values[n]), chosen)
        return chosen

    def first_step(self, value, total):
        laplace = total - 6.0 * value
        force = diffusion * laplace + reaction * value * (1.0 - value * value)
        for n in range(self.nodes):
            right = (value + self.whole[n] * force - self.stiffness[n] * laplace) * self.scales[n]
            yield n, right, value + (self.whole[n] * self.scales[n]) * force

    def second_step(self, node, start, steps):
        stiffness = self.own(node, self.stiffness)
        scale = self.own(node, self.scales)
        integral = start
        own_value, own_laplace = None, None
        for n, (_, value, total) in enumerate(steps):
            laplace = total - 6.0 * value
            force = diffusion * laplace + reaction * value * (1.0 - value * value)
            weight = self.own(node, [self.weights[m, n] for m in range(self.nodes)])
            integral = integral + weight * force
            own_value = value if n == 0 else jnp.where(node == n, value, own_value)
            own_laplace = laplace if n == 0 else jnp.where(node == n, laplace, own_laplace)
        right = (integral - stiffness * own_laplace) * scale
        return right, (integral + (6.0 * stiffness) * own_value) * scale

    def factor(self, node, sweep, n):
        if sweep == 0:
            return self.stiffness[n] * self.scales[n]
        return self.own(node, self.stiffness) * self.own(node, self.scales)


def near_kernel(scheme, chip_half, far_half, chip_got, table, edges, mirror, planes, sums, lanes, state):
    sub = lax.axis_index("sub")
    node = lax.axis_index("node")
    nodes = scheme.nodes
    routes = lane_routes(table, sub)
    for index, route in enumerate(routes):
        lanes[index] = route
    faces = face_routes(routes)
    below, above = slice(0, 8), slice(16, 24)
    low_half = pl.ds(pl.multiple_of(sub * 16, 8), 8)
    chip_half_rows = pl.ds(8, 8)
    high_half = pl.ds(pl.multiple_of(16 - sub * 16, 8), 8)

    def store_far(cell, value):
        state[0, cell, low_half] = value
        edges[0, cell, above] = value
        edges[0, cell, below] = value

    def store_chip(cell, value):
        state[0, cell, chip_half_rows] = value

    def store_got(cell, value):
        state[0, cell, high_half] = value

    spread(far_half, store_far)
    spread(chip_half, store_chip)
    spread_to(chip_got, routes[4], store_got)
    for row in range(8):
        mirror[:, 7 - row : 8 - row, :] = edges[0, :, row : row + 1, :]

    span = EDGE + 8

    def starts(level):
        count = -(-(span - 2 * level) // 8)
        if count == 1:
            return [level]
        return [level + round(piece * (span - 2 * level - 8) / (count - 1)) for piece in range(count)]

    def keep(index, level, start, cell, value):
        state[index, cell, pl.ds(start, 8)] = value
        if start == level:
            edges[index, cell, above] = value
        if start == span - 8 - level:
            edges[index, cell, below] = value

    for start in starts(1):
        for cell, value, total in around_at(state.at[0], start, 1, faces):
            for n, right, update in scheme.first_step(value, total):
                keep(scheme.right(0, n), 1, start, cell, right)
                keep(scheme.field(1, n), 1, start, cell, update)
    for level in range(2, JACOBI + 1):
        for start in starts(level):
            for n in range(nodes):
                factor = scheme.factor(node, 0, n)
                for cell, value, total in around_at(state.at[scheme.field(level - 1, n)], start, 1, faces):
                    right = state[scheme.right(0, n), cell, pl.ds(start, 8)]
                    keep(scheme.field(level, n), level, start, cell, right + factor * total)
    level = JACOBI + 1
    for start in starts(level):
        sources = [state.at[scheme.field(JACOBI, n)] for n in range(nodes)]
        for steps in zip(*[around_at(source, start, 1, faces) for source in sources]):
            cell = steps[0][0]
            right, update = scheme.second_step(node, state[0, cell, pl.ds(start, 8)], steps)
            keep(scheme.right(1), level, start, cell, right)
            keep(scheme.field(level), level, start, cell, update)
    factor = scheme.factor(node, 1, 0)
    for level in range(JACOBI + 2, 2 * JACOBI):
        for start in starts(level):
            for cell, value, total in around_at(state.at[scheme.field(level - 1)], start, 1, faces):
                right = state[scheme.right(1), cell, pl.ds(start, 8)]
                keep(scheme.field(level), level, start, cell, right + factor * total)
    first_squares, second_squares = [], []
    start = 2 * JACOBI
    rows = pl.ds(start, 8)
    earlier_place = scheme.field(JACOBI) + node
    for cell, value, total in around_at(state.at[scheme.field(start - 1)], start, 1, faces):
        update = state[scheme.right(1), cell, rows] + factor * total
        planes[cell] = update
        earlier = state[earlier_place, cell, rows]
        change = update - earlier
        second_squares.append(change * change)
        change = earlier - state[0, cell, rows]
        first_squares.append(change * change)
    sums[0] = added(first_squares)
    sums[1] = added(second_squares)


def far_kernel(scheme, far_got, edges, mirror, near_sums, lanes, planes, sums, state):
    sub = lax.axis_index("sub")
    for side in range(2):

        @pl.when(sub == side)
        def _():
            far_side(scheme, side, far_got, mirror, near_sums, lanes, planes, sums, state)


def far_side(scheme, side, far_got, mirror, near_sums, lanes, planes, sums, state):
    curve = lax.axis_index("curve")
    node = lax.axis_index("node")
    nodes = scheme.nodes
    faces = face_routes([lanes[index] for index in range(4)])
    toward = 1 - 2 * side
    at_end = curve == (0 if side == 0 else lax.axis_size("curve") - 1)
    new = pl.ds(8, 8)

    def store_far(cell, value):
        state[0, cell, new] = jnp.where(at_end, mirror[cell], value)

    spread_to(far_got, lanes[5], store_far)

    def shifted(levels):
        return pl.ds(8 + toward * levels, 8)

    def ring(index):
        source = state.at[index]
        return around(
            lambda cell: source[cell, shifted(1)],
            lambda cell: source[cell, new],
            lambda cell: source[cell, shifted(2)],
            faces,
        )

    def write(pending):
        for index, cell, value in pending:
            state[index, cell, new] = value

    pending = []
    for cell, value, total in ring(0):
        for n, right, update in scheme.first_step(value, total):
            pending.append((scheme.right(0, n), cell, right))
            pending.append((scheme.field(1, n), cell, update))
    write(pending)
    for level in range(2, JACOBI + 1):
        pending = []
        for n in range(nodes):
            factor = scheme.factor(node, 0, n)
            for cell, value, total in ring(scheme.field(level - 1, n)):
                right = state[scheme.right(0, n), cell, shifted(level - 1)]
                pending.append((scheme.field(level, n), cell, right + factor * total))
        write(pending)
    level = JACOBI + 1
    pending = []
    for steps in zip(*[ring(scheme.field(JACOBI, n)) for n in range(nodes)]):
        cell = steps[0][0]
        right, update = scheme.second_step(node, state[0, cell, shifted(level)], steps)
        pending.append((scheme.right(1), cell, right))
        pending.append((scheme.field(level), cell, update))
    write(pending)
    factor = scheme.factor(node, 1, 0)
    for level in range(JACOBI + 2, 2 * JACOBI):
        pending = []
        for cell, value, total in ring(scheme.field(level - 1)):
            right = state[scheme.right(1), cell, shifted(level - JACOBI - 1)]
            pending.append((scheme.field(level), cell, right + factor * total))
        write(pending)
    level = 2 * JACOBI
    first_squares, second_squares = [near_sums[0]], [near_sums[1]]
    for cell, value, total in ring(scheme.field(level - 1)):
        update = state[scheme.right(1), cell, shifted(JACOBI - 1)] + factor * total
        planes[cell] = update
        earlier = state[scheme.field(JACOBI) + node, cell, shifted(JACOBI)]
        change = update - earlier
        second_squares.append(change * change)
        change = earlier - state[0, cell, shifted(level)]
        first_squares.append(change * change)
    sums[0:1, :] = jnp.sum(added(first_squares), axis=0, keepdims=True)
    sums[1:2, :] = jnp.sum(added(second_squares), axis=0, keepdims=True)


def norm_kernel(cells, sums, got, norms):
    totals = jnp.sum(sums[...] + got[...], axis=1, keepdims=True)
    lane = lax.broadcasted_iota(jnp.int32, (1, 2), 1)
    norms[...] = jnp.sqrt(jnp.where(lane == 0, totals[0:1], totals[1:2]) / cells + 1e-06)


def added(terms):
    while len(terms) > 1:
        terms = [sum(terms[place + 1 : place + 2], terms[place]) for place in range(0, len(terms), 2)]
    return terms[0]


def pairs_over(sizes, partner):
    pairs = []
    for index in np.ndindex(*sizes):
        other = partner(*[int(i) for i in index])
        if other is not None:
            pairs.append((int(np.ravel_multi_index(index, sizes)), int(np.ravel_multi_index(other, sizes))))
    return pairs


def shards(start_field, neighbours):
    nodes = lax.axis_size("node")
    axes = ("slab", "curve", "node", "sub")
    sizes = tuple(lax.axis_size(axis) for axis in axes)
    chips = sizes[1]
    scheme = Scheme(nodes, *radau_tables(nodes))
    half = jax.ShapeDtypeStruct((8, 8, EDGE * EDGE), jnp.float32)
    planes = jax.ShapeDtypeStruct((CELLS, 8, LANES), jnp.float32)
    limit = pltpu.CompilerParams(vmem_limit_bytes=24 * 1024 * 1024)

    def across(slab, curve, node, sub):
        if sub == 1 and curve + 1 < chips:
            return (slab, curve + 1, node, 0)
        if sub == 0 and curve > 0:
            return (slab, curve - 1, node, 1)
        return (slab ^ 1, curve, node, sub) if slab ^ 1 < sizes[0] else None

    def beside(bit, swap):
        def partner(slab, curve, node, sub):
            return (slab, curve ^ bit, node, sub ^ swap)

        return partner

    def moved(value, partner):
        return lax.ppermute(value, axes, pairs_over(sizes, partner))

    far_half, chip_half = pl.pallas_call(
        halves_kernel,
        out_shape=[half, half],
        in_specs=[pl.BlockSpec(memory_space=pltpu.HBM)],
        out_specs=[VMEM, VMEM],
        scratch_shapes=[pltpu.SemaphoreType.DMA, pltpu.SemaphoreType.DMA],
        compiler_params=limit,
    )(start_field)
    far_got = moved(far_half, across)
    chip_got = moved(chip_half, beside(0, 1))
    shared = jax.ShapeDtypeStruct((scheme.count, CELLS, EDGE + 8, LANES), jnp.float32)
    edges, mirror, near_planes, near_sums, lanes = pl.pallas_call(
        functools.partial(near_kernel, scheme),
        out_shape=[
            shared,
            planes,
            planes,
            jax.ShapeDtypeStruct((2, 8, LANES), jnp.float32),
            jax.ShapeDtypeStruct((6, 8, LANES), jnp.int32),
        ],
        in_specs=[VMEM] * 4,
        out_specs=[VMEM] * 5,
        scratch_shapes=[pltpu.VMEM(shared.shape, jnp.float32)],
        compiler_params=limit,
        cost_estimate=pl.CostEstimate(flops=8_000_000, bytes_accessed=2_000_000, transcendentals=0),
    )(chip_half, far_half, chip_got, neighbours)
    far_planes, sums, _ = pl.pallas_call(
        functools.partial(far_kernel, scheme),
        out_shape=[planes, jax.ShapeDtypeStruct((2, LANES), jnp.float32), shared],
        in_specs=[VMEM] * 5,
        out_specs=[VMEM] * 3,
        input_output_aliases={1: 2},
        compiler_params=limit,
    )(far_got, edges, mirror, near_sums, lanes)
    field = pl.pallas_call(
        merge_kernel,
        out_shape=jax.ShapeDtypeStruct((1, 8, EDGE, EDGE * EDGE), jnp.float32),
        in_specs=[VMEM, VMEM],
        out_specs=VMEM,
        compiler_params=limit,
    )(near_planes, far_planes)
    rounds = [beside(0, 1)]
    bit = 1
    while bit < chips:
        rounds.append(beside(bit, 1))
        bit *= 2
    for partner in rounds[:-1]:
        sums = sums + moved(sums, partner)
    cells = start_field.size * chips * sizes[3]
    increments = pl.pallas_call(
        functools.partial(norm_kernel, np.float32(cells)),
        out_shape=jax.ShapeDtypeStruct((1, SWEEPS), jnp.float32),
        in_specs=[VMEM, VMEM],
        out_specs=VMEM,
        compiler_params=limit,
    )(sums, moved(sums, rounds[-1]))
    return (field, increments.T)


def solution(mesh):
    placed = (P(("slab", "curve", "sub"), None, None), P(("slab", "curve", "sub"), None))
    return jax.shard_map(
        shards,
        mesh=mesh,
        in_specs=placed,
        out_specs=(P("node", ("slab", "curve", "sub"), None, None), P("slab", "node")),
        check_vma=False,
    )
```

```python
import functools

import jax
import jax.numpy as jnp
import numpy as np
from jax import lax
from jax.experimental import pallas as pl
from jax.experimental.pallas import tpu as pltpu
from jax.sharding import PartitionSpec as P

SWEEPS = 2
JACOBI = 4

diffusion = 0.5
reaction = 1.0
EDGE = 16
LANES = 128
CELLS = 16
SWAPS = ((4, 5), (2, 4), (1, 1), (8, 0))
VMEM = pl.BlockSpec(memory_space=pltpu.VMEM)


def legendre_value(order, place):
    before = 1.0
    current = place
    for degree in range(1, order):
        following = ((2 * degree + 1) * place * current - degree * before) / (degree + 1)
        before = current
        current = following
    return current


def radau_residue(node_count, moment):
    place = 2.0 * moment - 1.0
    return legendre_value(node_count, place) - legendre_value(node_count - 1, place)


def radau_tables(node_count):
    samples = 4000
    points = []
    for sample in range(samples - 1):
        left_end = sample / samples
        right_end = (sample + 1) / samples
        left_value = radau_residue(node_count, left_end)
        right_value = radau_residue(node_count, right_end)
        if left_value * right_value < 0.0:
            for halving in range(80):
                middle = 0.5 * (left_end + right_end)
                middle_value = radau_residue(node_count, middle)
                if left_value * middle_value <= 0.0:
                    right_end = middle
                else:
                    left_end = middle
                    left_value = middle_value
            points.append(0.5 * (left_end + right_end))
    points.append(1.0)
    table = []
    for row_node in range(node_count):
        table_row = []
        for col_node in range(node_count):
            factors = [1.0]
            for other_node in range(node_count):
                if other_node != col_node:
                    scale = 1.0 / (points[col_node] - points[other_node])
                    shifted = [0.0] + factors
                    product = [
                        shifted[place]
                        - points[other_node] * (factors[place] if place < len(factors) else 0.0)
                        for place in range(len(shifted))
                    ]
                    factors = [entry * scale for entry in product]
            integral = 0.0
            for power_index in range(len(factors)):
                integral = integral + factors[power_index] * points[row_node] ** (
                    power_index + 1
                ) / (power_index + 1)
            table_row.append(integral)
        table.append(table_row)
    return (np.array(table, dtype=np.float32), np.array(points, dtype=np.float32))


def swap_bits(values):
    lane = lax.broadcasted_iota(jnp.int32, (8, LANES), 1)
    for register_bit, lane_bit in SWAPS:
        shift = 1 << lane_bit
        high = (lane >> lane_bit) & 1 == 1
        out = list(values)
        for index in range(CELLS):
            if index & register_bit == 0:
                low_value, high_value = values[index], values[index | register_bit]
                out[index] = jnp.where(high, pltpu.roll(high_value, shift, 1), low_value)
                out[index | register_bit] = jnp.where(
                    high, high_value, pltpu.roll(low_value, LANES - shift, 1)
                )
        values = out
    return values


def cell_of(index):
    return ((index >> 1) & 3) * 4 + ((index & 1) << 1 | index >> 3)


def spread(source, store):
    values = [source[index & 7, :, (index >> 3) * LANES : (index >> 3) * LANES + LANES] for index in range(CELLS)]
    for index, value in enumerate(swap_bits(values)):
        store(cell_of(index), value)


def spread_to(source, route, store):
    lane = lax.broadcasted_iota(jnp.int32, (8, LANES), 1)
    values = [source[index & 7, :, (index >> 3) * LANES : (index >> 3) * LANES + LANES] for index in range(CELLS)]
    for stage, origin in ((0, None), (2, route)):
        (bit_a, lane_a), (bit_b, lane_b) = SWAPS[stage : stage + 2]
        spot = lane if origin is None else origin
        high_a = (spot >> lane_a) & 1 == 1
        high_b = (spot >> lane_b) & 1 == 1
        shifts = {}

        def moved_by(value, step_a, step_b):
            shift = step_a * (1 << lane_a) + step_b * (1 << lane_b)
            if origin is None:
                return value if shift == 0 else pltpu.roll(value, -shift % LANES, 1)
            if shift not in shifts:
                shifts[shift] = (origin + shift) & (LANES - 1)
            return picked(value, shifts[shift])

        out = []
        for index in range(CELLS):
            base = index & ~(bit_a | bit_b)
            own_a, own_b = int(index & bit_a != 0), int(index & bit_b != 0)
            parts = [
                [moved_by(values[base | p * bit_a | q * bit_b], own_a - p, own_b - q) for q in range(2)]
                for p in range(2)
            ]
            rows = [jnp.where(high_b, part[1], part[0]) for part in parts]
            out.append(jnp.where(high_a, rows[1], rows[0]))
        values = out
    for index, value in enumerate(values):
        store(cell_of(index), value)


def lane_of(slot, outer_j, outer_k):
    return (
        (outer_j & 1) << 6
        | (slot >> 2) << 5
        | ((slot >> 1) & 1) << 4
        | outer_k << 2
        | (slot & 1) << 1
        | outer_j >> 1
    )


def lane_routes(table, sub):
    lane = lax.broadcasted_iota(jnp.int32, (8, LANES), 1)
    row = lax.broadcasted_iota(jnp.int32, (8, LANES), 0)
    slot = ((lane >> 5) & 1) << 2 | ((lane >> 4) & 1) << 1 | (lane >> 1) & 1
    outer_j = (lane & 1) << 1 | lane >> 6
    outer_k = (lane >> 2) & 3
    named = []
    for face in range(6):
        column = jnp.broadcast_to(table[:, face : face + 1], (8, LANES))
        picked = jnp.sum(jnp.where(slot == row, column, 0), axis=0, keepdims=True)
        named.append(jnp.broadcast_to(picked, (8, LANES)))

    def inside(edge, face, within, wrapped):
        other = lane_of(named[face] & 7, *wrapped)
        other = jnp.where(named[face] < 0, LANES, other)
        return jnp.where(edge, other, lane_of(slot, *within))

    routes = [
        inside(outer_j == 0, 2, (outer_j - 1, outer_k), (3, outer_k)),
        inside(outer_j == 3, 3, (outer_j + 1, outer_k), (0, outer_k)),
        inside(outer_k == 0, 4, (outer_j, outer_k - 1), (outer_j, 3)),
        inside(outer_k == 3, 5, (outer_j, outer_k + 1), (outer_j, 0)),
    ]
    low = lane_of(named[0] & 7, outer_j, outer_k)
    high = lane_of(named[1] & 7, outer_j, outer_k)
    routes.append(jnp.where(sub == 0, high, low))
    routes.append(jnp.where(sub == 0, low, high))
    return routes


def picked(value, lanes):
    return jnp.take_along_axis(value, lanes, axis=1, mode="promise_in_bounds")


def halves_kernel(field, far_half, chip_half, far_done, chip_done):
    sub = lax.axis_index("sub")
    moves = []
    for target, start, done in (
        (far_half, sub * 8, far_done),
        (chip_half, 8 - sub * 8, chip_done),
    ):
        rows = pl.ds(pl.multiple_of(start, 8), 8)
        move = pltpu.make_async_copy(field.at[:, rows, :], target, done)
        move.start()
        moves.append(move)
    for move in moves:
        move.wait()


def merge_kernel(near, far, field):
    sub = lax.axis_index("sub")
    for planes, start in ((near, 8 - sub * 8), (far, sub * 8)):
        rows = pl.ds(pl.multiple_of(start, 8), 8)
        values = swap_bits([planes[cell_of(index)] for index in range(CELLS)])
        for index, value in enumerate(values):
            columns = slice((index >> 3) * LANES, (index >> 3) * LANES + LANES)
            field[0, index & 7, rows, columns] = value


def face_routes(routes):
    return [(route < LANES, route & (LANES - 1)) for route in routes[:4]]


def around(center, side_a, side_b, faces):
    def across(face, own, other):
        inner, lanes = faces[face]
        return jnp.where(inner, picked(other, lanes), own)

    cells = [center(cell) for cell in range(CELLS)]
    for cell in range(CELLS):
        value = cells[cell]
        inner_j, inner_k = cell // 4, cell % 4
        total = side_a(cell) + side_b(cell)
        below = cells[cell - 4] if inner_j > 0 else across(0, value, cells[cell + 12])
        above = cells[cell + 4] if inner_j < 3 else across(1, value, cells[cell - 12])
        before = cells[cell - 1] if inner_k > 0 else across(2, value, cells[cell + 3])
        behind = cells[cell + 1] if inner_k < 3 else across(3, value, cells[cell - 3])
        yield cell, value, (total + (below + above)) + (before + behind)


def around_at(source, start, step, faces):
    return around(
        lambda cell: source[cell, pl.ds(start, 8)],
        lambda cell: source[cell, pl.ds(start - step, 8)],
        lambda cell: source[cell, pl.ds(start + step, 8)],
        faces,
    )


class Scheme:
    def __init__(self, nodes, weights, points):
        one, six = np.float32(1.0), np.float32(6.0)
        self.nodes = nodes
        self.weights = weights
        self.stiffness = [np.float32(diffusion) * points[n] for n in range(nodes)]
        self.scales = [one / (one + six * a) for a in self.stiffness]
        self.whole = [np.float32(np.sum(weights[n].astype(np.float64))) for n in range(nodes)]
        self.count = 5 * nodes + 5

    def field(self, level, node=0):
        if level == 0:
            return 0
        if level <= JACOBI:
            return 1 + (level - 1) * self.nodes + node
        return JACOBI * self.nodes + level - JACOBI

    def right(self, sweep, node=0):
        return JACOBI * self.nodes + JACOBI + (node if sweep == 0 else self.nodes)

    def own(self, node, values):
        chosen = jnp.float32(values[0])
        for n in range(1, self.nodes):
            chosen = jnp.where(node == n, jnp.float32(values[n]), chosen)
        return chosen

    def first_step(self, value, total):
        laplace = total - 6.0 * value
        force = diffusion * laplace + reaction * value * (1.0 - value * value)
        for n in range(self.nodes):
            right = (value + self.whole[n] * force - self.stiffness[n] * laplace) * self.scales[n]
            yield n, right, value + (self.whole[n] * self.scales[n]) * force

    def second_step(self, node, start, steps):
        stiffness = self.own(node, self.stiffness)
        scale = self.own(node, self.scales)
        integral = start
        own_value, own_laplace = None, None
        for n, (_, value, total) in enumerate(steps):
            laplace = total - 6.0 * value
            force = diffusion * laplace + reaction * value * (1.0 - value * value)
            weight = self.own(node, [self.weights[m, n] for m in range(self.nodes)])
            integral = integral + weight * force
            own_value = value if n == 0 else jnp.where(node == n, value, own_value)
            own_laplace = laplace if n == 0 else jnp.where(node == n, laplace, own_laplace)
        right = (integral - stiffness * own_laplace) * scale
        return right, (integral + (6.0 * stiffness) * own_value) * scale

    def factor(self, node, sweep, n):
        if sweep == 0:
            return self.stiffness[n] * self.scales[n]
        return self.own(node, self.stiffness) * self.own(node, self.scales)


def near_kernel(scheme, chip_half, far_half, chip_got, table, edges, mirror, planes, sums, lanes, state):
    sub = lax.axis_index("sub")
    node = lax.axis_index("node")
    nodes = scheme.nodes
    routes = lane_routes(table, sub)
    for index, route in enumerate(routes):
        lanes[index] = route
    faces = face_routes(routes)
    below, above = slice(0, 8), slice(16, 24)
    low_half = pl.ds(pl.multiple_of(sub * 16, 8), 8)
    chip_half_rows = pl.ds(8, 8)
    high_half = pl.ds(pl.multiple_of(16 - sub * 16, 8), 8)

    def store_far(cell, value):
        state[0, cell, low_half] = value
        edges[0, cell, above] = value
        edges[0, cell, below] = value

    def store_chip(cell, value):
        state[0, cell, chip_half_rows] = value

    def store_got(cell, value):
        state[0, cell, high_half] = value

    spread(far_half, store_far)
    spread(chip_half, store_chip)
    spread_to(chip_got, routes[4], store_got)
    for row in range(8):
        mirror[:, 7 - row : 8 - row, :] = edges[0, :, row : row + 1, :]

    span = EDGE + 8

    def starts(level):
        count = -(-(span - 2 * level) // 8)
        if count == 1:
            return [level]
        return [level + round(piece * (span - 2 * level - 8) / (count - 1)) for piece in range(count)]

    def keep(index, level, start, cell, value):
        state[index, cell, pl.ds(start, 8)] = value
        if start == level:
            edges[index, cell, above] = value
        if start == span - 8 - level:
            edges[index, cell, below] = value

    for start in starts(1):
        for cell, value, total in around_at(state.at[0], start, 1, faces):
            for n, right, update in scheme.first_step(value, total):
                keep(scheme.right(0, n), 1, start, cell, right)
                keep(scheme.field(1, n), 1, start, cell, update)
    for level in range(2, JACOBI + 1):
        for start in starts(level):
            for n in range(nodes):
                factor = scheme.factor(node, 0, n)
                for cell, value, total in around_at(state.at[scheme.field(level - 1, n)], start, 1, faces):
                    right = state[scheme.right(0, n), cell, pl.ds(start, 8)]
                    keep(scheme.field(level, n), level, start, cell, right + factor * total)
    level = JACOBI + 1
    for start in starts(level):
        sources = [state.at[scheme.field(JACOBI, n)] for n in range(nodes)]
        for steps in zip(*[around_at(source, start, 1, faces) for source in sources]):
            cell = steps[0][0]
            right, update = scheme.second_step(node, state[0, cell, pl.ds(start, 8)], steps)
            keep(scheme.right(1), level, start, cell, right)
            keep(scheme.field(level), level, start, cell, update)
    factor = scheme.factor(node, 1, 0)
    for level in range(JACOBI + 2, 2 * JACOBI):
        for start in starts(level):
            for cell, value, total in around_at(state.at[scheme.field(level - 1)], start, 1, faces):
                right = state[scheme.right(1), cell, pl.ds(start, 8)]
                keep(scheme.field(level), level, start, cell, right + factor * total)
    first_squares, second_squares = [], []
    start = 2 * JACOBI
    rows = pl.ds(start, 8)
    earlier_place = scheme.field(JACOBI) + node
    for cell, value, total in around_at(state.at[scheme.field(start - 1)], start, 1, faces):
        update = state[scheme.right(1), cell, rows] + factor * total
        planes[cell] = update
        earlier = state[earlier_place, cell, rows]
        change = update - earlier
        second_squares.append(change * change)
        change = earlier - state[0, cell, rows]
        first_squares.append(change * change)
    sums[0] = added(first_squares)
    sums[1] = added(second_squares)


def far_kernel(scheme, far_got, edges, mirror, near_sums, lanes, planes, sums, state):
    sub = lax.axis_index("sub")
    for side in range(2):

        @pl.when(sub == side)
        def _():
            far_side(scheme, side, far_got, mirror, near_sums, lanes, planes, sums, state)


def far_side(scheme, side, far_got, mirror, near_sums, lanes, planes, sums, state):
    curve = lax.axis_index("curve")
    node = lax.axis_index("node")
    nodes = scheme.nodes
    faces = face_routes([lanes[index] for index in range(4)])
    toward = 1 - 2 * side
    at_end = curve == (0 if side == 0 else lax.axis_size("curve") - 1)
    new = pl.ds(8, 8)

    def store_far(cell, value):
        state[0, cell, new] = jnp.where(at_end, mirror[cell], value)

    spread_to(far_got, lanes[5], store_far)

    def shifted(levels):
        return pl.ds(8 + toward * levels, 8)

    def ring(index):
        source = state.at[index]
        return around(
            lambda cell: source[cell, shifted(1)],
            lambda cell: source[cell, new],
            lambda cell: source[cell, shifted(2)],
            faces,
        )

    def write(pending):
        for index, cell, value in pending:
            state[index, cell, new] = value

    pending = []
    for cell, value, total in ring(0):
        for n, right, update in scheme.first_step(value, total):
            pending.append((scheme.right(0, n), cell, right))
            pending.append((scheme.field(1, n), cell, update))
    write(pending)
    for level in range(2, JACOBI + 1):
        pending = []
        for n in range(nodes):
            factor = scheme.factor(node, 0, n)
            for cell, value, total in ring(scheme.field(level - 1, n)):
                right = state[scheme.right(0, n), cell, shifted(level - 1)]
                pending.append((scheme.field(level, n), cell, right + factor * total))
        write(pending)
    level = JACOBI + 1
    pending = []
    for steps in zip(*[ring(scheme.field(JACOBI, n)) for n in range(nodes)]):
        cell = steps[0][0]
        right, update = scheme.second_step(node, state[0, cell, shifted(level)], steps)
        pending.append((scheme.right(1), cell, right))
        pending.append((scheme.field(level), cell, update))
    write(pending)
    factor = scheme.factor(node, 1, 0)
    for level in range(JACOBI + 2, 2 * JACOBI):
        pending = []
        for cell, value, total in ring(scheme.field(level - 1)):
            right = state[scheme.right(1), cell, shifted(level - JACOBI - 1)]
            pending.append((scheme.field(level), cell, right + factor * total))
        write(pending)
    level = 2 * JACOBI
    first_squares, second_squares = [near_sums[0]], [near_sums[1]]
    for cell, value, total in ring(scheme.field(level - 1)):
        update = state[scheme.right(1), cell, shifted(JACOBI - 1)] + factor * total
        planes[cell] = update
        earlier = state[scheme.field(JACOBI) + node, cell, shifted(JACOBI)]
        change = update - earlier
        second_squares.append(change * change)
        change = earlier - state[0, cell, shifted(level)]
        first_squares.append(change * change)
    sums[0:1, :] = jnp.sum(added(first_squares), axis=0, keepdims=True)
    sums[1:2, :] = jnp.sum(added(second_squares), axis=0, keepdims=True)


def norm_kernel(cells, sums, got, norms):
    totals = jnp.sum(sums[...] + got[...], axis=1, keepdims=True)
    lane = lax.broadcasted_iota(jnp.int32, (1, 2), 1)
    norms[...] = jnp.sqrt(jnp.where(lane == 0, totals[0:1], totals[1:2]) / cells + 1e-06)


def added(terms):
    while len(terms) > 1:
        terms = [sum(terms[place + 1 : place + 2], terms[place]) for place in range(0, len(terms), 2)]
    return terms[0]


def pairs_over(sizes, partner):
    pairs = []
    for index in np.ndindex(*sizes):
        other = partner(*[int(i) for i in index])
        if other is not None:
            pairs.append((int(np.ravel_multi_index(index, sizes)), int(np.ravel_multi_index(other, sizes))))
    return pairs


def shards(start_field, neighbours):
    nodes = lax.axis_size("node")
    axes = ("curve", "node", "sub")
    sizes = tuple(lax.axis_size(axis) for axis in axes)
    chips = sizes[0]
    scheme = Scheme(nodes, *radau_tables(nodes))
    half = jax.ShapeDtypeStruct((8, 8, EDGE * EDGE), jnp.float32)
    planes = jax.ShapeDtypeStruct((CELLS, 8, LANES), jnp.float32)
    limit = pltpu.CompilerParams(vmem_limit_bytes=24 * 1024 * 1024)

    def across(curve, node, sub):
        if sub == 1 and curve + 1 < chips:
            return (curve + 1, node, 0)
        if sub == 0 and curve > 0:
            return (curve - 1, node, 1)
        return (curve, node ^ 1, sub) if node ^ 1 < nodes else None

    def beside(bit, swap):
        def partner(curve, node, sub):
            return (curve ^ bit, node, sub ^ swap)

        return partner

    def moved(value, partner):
        return lax.ppermute(value, axes, pairs_over(sizes, partner))

    far_half, chip_half = pl.pallas_call(
        halves_kernel,
        out_shape=[half, half],
        in_specs=[pl.BlockSpec(memory_space=pltpu.HBM)],
        out_specs=[VMEM, VMEM],
        scratch_shapes=[pltpu.SemaphoreType.DMA, pltpu.SemaphoreType.DMA],
        compiler_params=pltpu.CompilerParams(vmem_limit_bytes=55040 * 1024),
    )(start_field)
    far_got = moved(far_half, across)
    chip_got = moved(chip_half, beside(0, 1))
    shared = jax.ShapeDtypeStruct((scheme.count, CELLS, EDGE + 8, LANES), jnp.float32)
    edges, mirror, near_planes, near_sums, lanes = pl.pallas_call(
        functools.partial(near_kernel, scheme),
        out_shape=[
            shared,
            planes,
            planes,
            jax.ShapeDtypeStruct((2, 8, LANES), jnp.float32),
            jax.ShapeDtypeStruct((6, 8, LANES), jnp.int32),
        ],
        in_specs=[VMEM] * 4,
        out_specs=[VMEM] * 5,
        scratch_shapes=[pltpu.VMEM(shared.shape, jnp.float32)],
        compiler_params=limit,
        cost_estimate=pl.CostEstimate(flops=8_000_000, bytes_accessed=2_000_000, transcendentals=0),
    )(chip_half, far_half, chip_got, neighbours)
    far_planes, sums, _ = pl.pallas_call(
        functools.partial(far_kernel, scheme),
        out_shape=[planes, jax.ShapeDtypeStruct((2, LANES), jnp.float32), shared],
        in_specs=[VMEM] * 5,
        out_specs=[VMEM] * 3,
        input_output_aliases={1: 2},
        compiler_params=limit,
    )(far_got, edges, mirror, near_sums, lanes)
    field = pl.pallas_call(
        merge_kernel,
        out_shape=jax.ShapeDtypeStruct((1, 8, EDGE, EDGE * EDGE), jnp.float32),
        in_specs=[VMEM, VMEM],
        out_specs=VMEM,
        compiler_params=limit,
    )(near_planes, far_planes)
    rounds = [beside(0, 1)]
    bit = 1
    while bit < chips:
        rounds.append(beside(bit, 1))
        bit *= 2
    for partner in rounds[:-1]:
        sums = sums + moved(sums, partner)
    cells = start_field.size * chips * sizes[2]
    increments = pl.pallas_call(
        functools.partial(norm_kernel, np.float32(cells)),
        out_shape=jax.ShapeDtypeStruct((1, SWEEPS), jnp.float32),
        in_specs=[VMEM, VMEM],
        out_specs=VMEM,
        compiler_params=limit,
    )(sums, moved(sums, rounds[-1]))
    return (field, increments.T)


def solution(mesh):
    placed = (P(("slab", "curve", "sub"), None, None), P(("slab", "curve", "sub"), None))
    return jax.shard_map(
        shards,
        mesh=mesh,
        in_specs=placed,
        out_specs=(P("node", ("slab", "curve", "sub"), None, None), P("slab", "node")),
        check_vma=False,
    )
```
